32 devices in a mesh: wide: 8 (over z, y), narrow: 4 (over x, core).
Axes of the slice: x: 2, y: 2, z: 4, core: 2. Of those that a mesh axis runs over, the one named last changes fastest.
Arguments:
- rhs: float32 [128, 32, 128], P('wide', 'narrow'), may hold values from -4 to 6
- coefficient: float32 [128, 32, 128], P('wide', 'narrow'), may hold values from 0.125 to 8
- guess: float32 [128, 32, 128], P('wide', 'narrow'), may hold values from -6 to 6
Outputs:
- pressure: float32 [128, 32, 128], P('wide', 'narrow')
- residual: float32 [128, 32, 128], P('wide', 'narrow')
The draws below stay inside these ranges and needn't reach their ends.
All inputs are finite; a program needn't handle non-finite values.
Results may differ from the reference program's by a relative error of at most 0.0003.
Values sent between devices are 32-bit elements; how exact they have to be, the bound alone decides.
A program may use at most 128 MiB of HBM per device.

```python
import math
import jax
import jax.numpy as jnp
from jax import lax

NY = 128
ITERS = 20
NX = 128
NZ = 32


def position_x():
    return (lax.broadcasted_iota(jnp.float32, (NX, NZ, NY), 0) + 0.5) / NX


def draw_coefficient(key, part):
    key = jax.random.fold_in(key, 11)
    place = position_x()
    ramp = jnp.exp(math.log(4.0) * (2.0 * place - 1.0))
    rough = jnp.exp(jax.random.uniform(key, (NX, NZ, NY), jnp.float32, math.log(0.5), math.log(2.0)))
    return ramp * rough


def draw_rhs(key, part):
    key = jax.random.fold_in(key, 23)
    place = position_x()
    smooth_part = 1.0 + 0.5 * jnp.cos(2.0 * math.pi * place)
    rough = jnp.clip(jax.random.normal(key, (NX, NZ, NY), jnp.float32), -4.0, 4.0) * 0.9
    return jnp.clip(rough + smooth_part, -4.0, 6.0)


def block_scale(stream_key, dims, shards, low, top_value):
    level = 1.0
    for position, parts in shards:
        heights = jax.random.uniform(jax.random.fold_in(jax.random.fold_in(stream_key, 6), position), (parts,), jnp.float32, low / len(shards), top_value / len(shards))
        level = level * jnp.repeat(jnp.exp(heights), dims[position] // parts).reshape((-1,) + (1,) * (len(dims) - 1 - position))
    return level


def normal_values(stream_key, shape, scale, most, shards=(), kind=jnp.bfloat16):
    entries = jax.random.normal(stream_key, shape, jnp.float32) * scale
    if len(shards) > 0:
        entries = block_scale(stream_key, shape, shards, -0.22, 0.18) * entries
    return jnp.clip(entries, min=-most, max=most).astype(kind)


def setup_inputs(seed: int = 0) -> dict:
    key_list = jax.random.split(jax.random.key(seed), 4)
    return {
        "rhs": draw_rhs(jax.random.fold_in(key_list[3], 71), 0),
        "coefficient": draw_coefficient(jax.random.fold_in(key_list[3], 71), 0),
        "guess": normal_values(key_list[2], (NX, NZ, NY), 1.0, 6.0, ((0, 8), (1, 4)), jnp.float32),
    }


def shifts(field):
    padded = jnp.pad(field, 1)
    return [padded[2:, 1:-1, 1:-1], padded[:-2, 1:-1, 1:-1], padded[1:-1, 2:, 1:-1],
            padded[1:-1, :-2, 1:-1], padded[1:-1, 1:-1, 2:], padded[1:-1, 1:-1, :-2]]


def weights(conduct):
    faces = [0.5 * (conduct + other) for other in shifts(conduct)]
    total = faces[0]
    for face in faces[1:]:
        total = total + face
    return faces, total


def beside_all(faces, field):
    near = shifts(field)
    total = faces[0] * near[0]
    for index in range(1, 6):
        total = total + faces[index] * near[index]
    return total


def restrict(field):
    sx, sz, sy = field.shape
    return jnp.sum(field.reshape(sx // 2, 2, sz // 2, 2, sy // 2, 2), axis=(1, 3, 5)) * 0.125


def prolong(field):
    return jnp.repeat(jnp.repeat(jnp.repeat(field, 2, axis=0), 2, axis=1), 2, axis=2)


def colours(shape):
    return (lax.broadcasted_iota(jnp.int32, shape, 0) + lax.broadcasted_iota(jnp.int32, shape, 1)
            + lax.broadcasted_iota(jnp.int32, shape, 2)) % 2


def smooth(field, source, faces, diag, scale, colour):
    for sweep in range(2):
        for parity in (0, 1):
            fresh = (source / scale + beside_all(faces, field)) / diag
            field = jnp.where(colour == parity, fresh, field)
    return field


def defect(field, source, faces, diag, scale):
    return source - scale * (diag * field - beside_all(faces, field))


def bottom(source, faces, diag, scale):
    def advance(step, carry):
        answer, remain, search, norm_now = carry
        image = scale * (diag * search - beside_all(faces, search))
        alpha = norm_now / jnp.sum(search * image)
        answer = answer + alpha * search
        remain = remain - alpha * image
        norm_next = jnp.sum(remain * remain)
        search = remain + (norm_next / norm_now) * search
        return answer, remain, search, norm_next
    start = (jnp.zeros_like(source), source, source, jnp.sum(source * source))
    return lax.fori_loop(0, ITERS, advance, start)[0]


def reference(rhs, coefficient, guess):
    conducts = [coefficient]
    for level in range(3):
        conducts.append(restrict(conducts[-1]))
    operators = [weights(conduct) for conduct in conducts]
    field = guess
    source = rhs
    fields = []
    sources = []
    for level in range(3):
        scale = 0.25 ** level
        if level > 0:
            field = jnp.zeros_like(source)
        faces, diag = operators[level]
        colour = colours(source.shape)
        field = smooth(field, source, faces, diag, scale, colour)
        fields.append(field)
        sources.append(source)
        source = restrict(defect(field, source, faces, diag, scale))
    faces, diag = operators[3]
    correction = bottom(source, faces, diag, 0.25 ** 3)
    for level in (2, 1, 0):
        scale = 0.25 ** level
        faces, diag = operators[level]
        field = fields[level] + prolong(correction)
        field = smooth(field, sources[level], faces, diag, scale, colours(field.shape))
        correction = field
    faces, diag = operators[0]
    return field, defect(field, rhs, faces, diag, 1.0)
```

```python
import functools

import jax
import jax.numpy as jnp
from jax import lax
from jax.experimental import pallas as pl
from jax.experimental.pallas import tpu as pltpu
from jax.sharding import PartitionSpec as P

ITERS = 20
LANES = 128
DEEP = 5
SIDE = 8
PAD = 2
MESH = pl.DeviceIdType.MESH


def dot(a, b):
    return lax.dot_general(
        a, b, (((1,), (0,)), ((), ())), precision=lax.Precision.HIGHEST, preferred_element_type=jnp.float32
    )


def iota(shape, dim):
    return lax.broadcasted_iota(jnp.int32, shape, dim)


def one(cond):
    return jnp.where(cond, 1.0, 0.0).astype(jnp.float32)


def coarse_lane(lane, part, ny):
    shift = ny.bit_length() - 1
    z = part * (LANES // ny) + (lane >> shift)
    return (z >> 1) * (ny // 2) + ((lane & (ny - 1)) >> 1)


def down_lanes(part, ny):
    shape = (LANES, LANES)
    return one(iota(shape, 1) == coarse_lane(iota(shape, 0), part, ny))


def up_lanes(part, ny):
    shape = (LANES, LANES)
    return one(iota(shape, 0) == coarse_lane(iota(shape, 1), part, ny))


def down_rows(rows):
    shape = (rows // 2, rows)
    return one(iota(shape, 0) == (iota(shape, 1) >> 1))


def up_rows(rows, coarse, first):
    shape = (rows, coarse)
    return one(iota(shape, 1) == (iota(shape, 0) >> 1) + first)


class Level:
    def __init__(self, k, f, u, wx, wy, wzp, wzm, diag, inv, ny, first, last, off=0, odd=0):
        self.k, self.f, self.u = k, f, u
        self.wx, self.wy, self.wzp, self.wzm, self.diag, self.inv = wx, wy, wzp, wzm, diag, inv
        self.ny, self.first, self.last, self.off, self.odd = ny, first, last, off, odd
        self.rows = k.shape[1]
        self.tiles = k.shape[0]

    def above(self, here, after):
        if self.ny == LANES:
            return after
        lane = iota(here.shape, 1)
        step = LANES - self.ny
        return jnp.where(lane < step, pltpu.roll(here, step, 1), pltpu.roll(after, step, 1))

    def below(self, here, before):
        if self.ny == LANES:
            return before
        lane = iota(here.shape, 1)
        return jnp.where(lane >= self.ny, pltpu.roll(here, self.ny, 1), pltpu.roll(before, self.ny, 1))

    def operator(self):
        shape = (self.rows, LANES)
        row = iota(shape, 0)
        y = iota(shape, 1) & (self.ny - 1)
        zero = jnp.zeros(shape, jnp.float32)
        for t in range(self.first, self.last):
            k = self.k[t]
            after = self.k[t + 1] if t + 1 < self.tiles else zero
            before = self.k[t - 1] if t > 0 else zero
            xp = jnp.where(row == self.rows - 1, 0.0, pltpu.roll(k, self.rows - 1, 0))
            xm = jnp.where(row == 0, 0.0, pltpu.roll(k, 1, 0))
            yp = jnp.where(y == self.ny - 1, 0.0, pltpu.roll(k, LANES - 1, 1))
            ym = jnp.where(y == 0, 0.0, pltpu.roll(k, 1, 1))
            zp = self.above(k, after)
            zm = self.below(k, before)
            diag = 3.0 * k + 0.5 * (xp + xm + zp + zm + yp + ym)
            diag = jnp.where(diag > 0.0, diag, 1.0)
            live = k > 0.0

            def face(other):
                return jnp.where(live & (other > 0.0), 0.5 * (k + other), 0.0)

            self.wx[t] = face(xp)
            self.wy[t] = face(yp)
            self.wzp[t] = face(zp)
            self.wzm[t] = face(zm)
            self.diag[t] = diag
            self.inv[t] = 1.0 / diag

    def beside(self, t, here, after, before):
        wx = self.wx[t]
        wy = self.wy[t]
        total = wx * pltpu.roll(here, self.rows - 1, 0) + pltpu.roll(wx * here, 1, 0)
        total = total + (wy * pltpu.roll(here, LANES - 1, 1) + pltpu.roll(wy * here, 1, 1))
        return total + (self.wzp[t] * self.above(here, after) + self.wzm[t] * self.below(here, before))

    def around(self, t):
        here = self.u[t + self.off]
        after = self.u[t + 1 + self.off] if t + 1 < self.tiles else here
        before = self.u[t - 1 + self.off] if t > 0 else here
        return here, after, before

    def smooth(self):
        shape = (self.rows, LANES)
        shift = self.ny.bit_length() - 1
        lane = iota(shape, 1)
        place = iota(shape, 0) + (lane >> shift) + (lane & (self.ny - 1)) + self.odd

        @pl.loop(0, 4)
        def _(step):
            even = ((place + step) & 1) == 0
            other = ((place + step) & 1) == 1
            for t in range(self.first, self.last):
                here, after, before = self.around(t)
                fresh = (self.f[t] + self.beside(t, here, after, before)) * self.inv[t]
                mask = other if (self.ny == LANES and t % 2 == 1) else even
                self.u[t + self.off] = jnp.where(mask, fresh, here)

    def defect(self, t):
        here, after, before = self.around(t)
        return self.f[t] - (self.diag[t] * here - self.beside(t, here, after, before))


def kernel(wide, narrow, rhs, cond, guess, pressure, residual, *scratch):
    (p0, u0r, op0, a1, u1r, u1, op1, a2, own2, g2, u2, op2, a3, op3,
     send0, recv0, send1, recv1, send2, recv2) = scratch
    w = lax.axis_index("wide")
    n = lax.axis_index("narrow")
    bx, bz, _ = rhs.shape
    hx, hz = bx // 2, bz // 2
    own_z = pl.ds(DEEP, bz)
    own_x = pl.ds(SIDE, bx)
    tiles_own = hz // 2
    f32 = jnp.float32

    for ref in (p0, u0r, a1, u1r):
        ref[...] = jnp.zeros(ref.shape, f32)
    u1[...] = jnp.zeros(u1.shape, f32)

    def valid(dw):
        return (w + dw >= 0) & (w + dw < wide)

    def when(cond_, body):
        if cond_ is True:
            body()
        else:
            pl.when(cond_)(body)

    barrier = pltpu.get_barrier_semaphore()

    def greet(dev):
        pl.semaphore_signal(barrier, inc=1, device_id=dev, device_id_type=MESH)

    for j in range(1, narrow):
        greet((w, lax.rem(n + j, narrow)))
    for dw in (-1, 1):
        @pl.when(valid(dw))
        def _(dw=dw):
            for j in range(narrow):
                greet((w + dw, lax.rem(n + j, narrow)))

    @pl.loop(0, wide)
    def _(other):
        @pl.when((other < w - 1) | (other > w + 1))
        def _():
            greet((other, n))

    for z in range(bz):
        p0[0, DEEP + z, SIDE:SIDE + bx, :] = cond[:, z, :]
        p0[1, DEEP + z, SIDE:SIDE + bx, :] = rhs[:, z, :]
        p0[2, DEEP + z, SIDE:SIDE + bx, :] = guess[:, z, :]

    half = down_rows(bx)
    lanes0 = [down_lanes(i, LANES) for i in (0, 2)]

    def to_level_1(index, slices, factor):
        for tt in range(tiles_own):
            four = [slices[4 * tt + i] for i in range(4)]
            spread = dot(four[0] + four[1], lanes0[0]) + dot(four[2] + four[3], lanes0[1])
            a1[index, n * tiles_own + tt, SIDE:SIDE + hx, :] = factor * dot(half, spread)

    to_level_1(0, [p0[0, DEEP + z, SIDE:SIDE + bx, :] for z in range(bz)], 0.125)

    near = jnp.where(w > 0, 1, 0) + jnp.where(w < wide - 1, 1, 0)
    pl.semaphore_wait(barrier, (wide - 1 - near) + near * narrow + narrow - 1)

    zs = {1: (DEEP + bz - DEEP, 0, DEEP), -1: (DEEP, DEEP + bz, DEEP), 0: (DEEP, DEEP, bz)}
    xs = {1: (SIDE + bx - SIDE, 0, SIDE), -1: (SIDE, SIDE + bx, SIDE), 0: (SIDE, SIDE, bx)}
    around = [(dw, dn) for dw in (-1, 0, 1) for dn in (-1, 0, 1) if (dw, dn) != (0, 0)]

    def has(dw, dn):
        good = None
        if dw:
            good = valid(dw)
        if dn:
            zgood = (n + dn >= 0) & (n + dn < narrow)
            good = zgood if good is None else good & zgood
        return good

    def fine(which, dw, dn):
        src_z, dst_z, len_z = zs[dn]
        src_x, dst_x, len_x = xs[dw]
        ref = p0 if which == 0 else u0r
        lead = (slice(None),) if which == 0 else ()
        src = ref.at[lead + (pl.ds(src_z, len_z), pl.ds(src_x, len_x))]
        dst = ref.at[lead + (pl.ds(dst_z, len_z), pl.ds(dst_x, len_x))]
        mine = (dw + 1) * 3 + dn + 1
        theirs = (1 - dw) * 3 + 1 - dn
        return pltpu.make_async_remote_copy(
            src_ref=src, dst_ref=dst, send_sem=send0.at[which, mine], recv_sem=recv0.at[which, theirs],
            device_id=(w + dw, n + dn), device_id_type=MESH)

    def fine_in(which, dw, dn):
        _, dst_z, len_z = zs[-dn]
        _, dst_x, len_x = xs[-dw]
        ref = p0 if which == 0 else u0r
        lead = (slice(None),) if which == 0 else ()
        dst = ref.at[lead + (pl.ds(dst_z, len_z), pl.ds(dst_x, len_x))]
        mine = (dw + 1) * 3 + dn + 1
        return pltpu.make_async_remote_copy(
            src_ref=dst, dst_ref=dst, send_sem=send0.at[which, mine], recv_sem=recv0.at[which, mine],
            device_id=(w + dw, n + dn), device_id_type=MESH)

    def fine_start(which):
        for dw, dn in around:
            pl.when(has(dw, dn))(lambda dw=dw, dn=dn: fine(which, dw, dn).start())

    def fine_recv(which):
        for dw, dn in around:
            pl.when(has(dw, dn))(lambda dw=dw, dn=dn: fine_in(which, dw, dn).wait_recv())

    def fine_sent(which):
        for dw, dn in around:
            pl.when(has(dw, dn))(lambda dw=dw, dn=dn: fine(which, dw, dn).wait_send())

    mid = [(dw, j) for dw in (0, -1, 1) for j in range(narrow) if (dw, j) != (0, 0)]

    def mid_ref(which):
        return u1r if which == 2 else a1.at[which]

    def middle(which, dw, j):
        ref = mid_ref(which)
        tile = pl.ds(n * tiles_own, tiles_own)
        return pltpu.make_async_remote_copy(
            src_ref=ref.at[tile, pl.ds(SIDE, hx)], dst_ref=ref.at[tile, pl.ds(SIDE - dw * hx, hx)],
            send_sem=send1.at[which, dw + 1, j], recv_sem=recv1.at[which, 1 - dw, j],
            device_id=(w + dw, lax.rem(n + j, narrow)), device_id_type=MESH)

    def middle_in(which, dw, j):
        ref = mid_ref(which)
        src = lax.rem(n + narrow - j, narrow)
        dst = ref.at[pl.ds(src * tiles_own, tiles_own), pl.ds(SIDE + dw * hx, hx)]
        return pltpu.make_async_remote_copy(
            src_ref=dst, dst_ref=dst, send_sem=send1.at[which, dw + 1, j], recv_sem=recv1.at[which, dw + 1, j],
            device_id=(w + dw, src), device_id_type=MESH)

    def each_mid(fun):
        for dw, j in mid:
            if dw == 0:
                fun(dw, j)
            else:
                pl.when(valid(dw))(lambda dw=dw, j=j: fun(dw, j))

    def mid_start(which):
        each_mid(lambda dw, j: middle(which, dw, j).start())

    def mid_recv(which):
        each_mid(lambda dw, j: middle_in(which, dw, j).wait_recv())

    def mid_sent(which):
        each_mid(lambda dw, j: middle(which, dw, j).wait_send())

    def top(which, step):
        other = lax.rem(w + step, wide)
        return pltpu.make_async_remote_copy(
            src_ref=own2.at[which], dst_ref=g2.at[which, w], send_sem=send2.at[which, step],
            recv_sem=recv2.at[which, step], device_id=(other, n), device_id_type=MESH)

    def top_in(which, step):
        src = lax.rem(w + wide - step, wide)
        return pltpu.make_async_remote_copy(
            src_ref=own2.at[which], dst_ref=g2.at[which, src], send_sem=send2.at[which, step],
            recv_sem=recv2.at[which, step], device_id=(src, n), device_id_type=MESH)

    def each_top(fun):
        @pl.loop(1, wide)
        def _(step):
            fun(step)

    fine_start(0)
    mid_start(0)
    fine_recv(0)

    names = range(6)
    ny = LANES
    zero_level = Level(p0.at[0], p0.at[1], p0.at[2], *[op0.at[i] for i in names], LANES, 1, 2 * DEEP + bz - 1, odd=1)
    zero_level.operator()
    fine_sent(0)
    zero_level.smooth()
    to_level_1(1, [zero_level.defect(DEEP + z)[SIDE:SIDE + bx] for z in range(bz)], 0.5)
    mid_start(1)
    u0r[own_z, own_x, :] = p0[2, own_z, own_x, :]
    fine_start(1)

    ny1, ny2, ny3 = LANES // 2, LANES // 4, LANES // 8
    mid_recv(0)
    one_level = Level(a1.at[0], a1.at[1], u1, *[op1.at[i] for i in names], ny1, 0, a1.shape[1], off=PAD)
    rows2 = hx // 2
    lanes1 = [down_lanes(i, ny1) for i in range(4)]
    tiles2 = a1.shape[1] // 4

    def to_level_2(which, tiles, factor):
        shape = (tiles2 * rows2, hx)
        pack = None
        for big in range(tiles2):
            spread = dot(tiles[4 * big], lanes1[0])
            for i in range(1, 4):
                spread = spread + dot(tiles[4 * big + i], lanes1[i])
            place = one(iota(shape, 0) == (iota(shape, 1) >> 1) + big * rows2)
            part = dot(place, spread)
            pack = part if pack is None else pack + part
        pack = factor * pack
        own2[which] = pack
        g2[which, w] = pack

    to_level_2(0, [a1[0, t, SIDE:SIDE + hx, :] for t in range(a1.shape[1])], 0.125)
    each_top(lambda step: top(0, step).start())
    one_level.operator()
    mid_recv(1)
    one_level.smooth()
    to_level_2(1, [one_level.defect(t)[SIDE:SIDE + hx] for t in range(a1.shape[1])], 0.5)
    each_top(lambda step: top(1, step).start())
    u1r[pl.ds(n * tiles_own, tiles_own), SIDE:SIDE + hx, :] = u1[pl.ds(PAD + n * tiles_own, tiles_own), SIDE:SIDE + hx, :]
    mid_start(2)

    def unpack(which):
        for other in range(wide):
            for t in range(tiles2):
                a2[which, t, other * rows2:(other + 1) * rows2, :] = g2[which, other, t * rows2:(t + 1) * rows2, :]

    each_top(lambda step: top_in(0, step).wait_recv())
    unpack(0)
    two_level = Level(a2.at[0], a2.at[1], u2, *[op2.at[i] for i in names], ny2, 0, tiles2)
    two_level.operator()
    all2, all3 = a2.shape[2], a3.shape[2]
    half2 = down_rows(all2)
    lanes2 = [down_lanes(i, ny2) for i in range(tiles2)]

    def to_level_3(tiles, factor):
        spread = dot(tiles[0], lanes2[0])
        for i in range(1, tiles2):
            spread = spread + dot(tiles[i], lanes2[i])
        return factor * dot(half2, spread)

    a3[0, 0] = to_level_3([a2[0, t] for t in range(tiles2)], 0.125)
    last = Level(a3.at[0], a3.at[1], a3.at[1], *[op3.at[i] for i in names], ny3, 0, 1)
    last.operator()
    each_top(lambda step: top_in(1, step).wait_recv())
    unpack(1)
    u2[...] = jnp.zeros(u2.shape, f32)
    two_level.smooth()
    source = to_level_3([two_level.defect(t) for t in range(tiles2)], 0.5)

    def image(v):
        return last.diag[0] * v - last.beside(0, v, v, v)

    def total(v):
        return jnp.sum(jnp.sum(v, axis=0, keepdims=True), axis=1, keepdims=True)

    first_image = image(source)
    rr = total(source * source)
    alpha = rr / total(source * first_image)

    def advance(step, carry):
        answer, remain, search, moved, norm, alpha = carry
        answer = answer + alpha * search
        remain = remain - alpha * moved
        fresh = image(remain)
        norm_next = total(remain * remain)
        cross = total(remain * fresh)
        beta = norm_next / norm
        alpha_next = norm_next / (cross - beta * norm_next / alpha)
        search = remain + beta * search
        moved = fresh + beta * moved
        return answer, remain, search, moved, norm_next, alpha_next

    carry = (jnp.zeros_like(source), source, source, first_image, rr, alpha)
    carry = lax.fori_loop(0, ITERS - 1, advance, carry)
    solved = carry[0] + carry[5] * carry[2]

    wider = dot(up_rows(all2, all3, 0), solved)
    for t in range(tiles2):
        u2[t] = u2[t] + dot(wider, up_lanes(t, ny2))
    two_level.smooth()

    window = a1.shape[2]
    pick = up_rows(window, all2, w * rows2 - SIDE // 2)
    grown = [dot(pick, u2[t]) for t in range(tiles2)]
    mid_sent(2)
    mid_recv(2)
    ups1 = [up_lanes(i, ny1) for i in range(4)]
    for t in range(a1.shape[1]):
        u1[PAD + t] = u1r[t] + dot(grown[t // 4], ups1[t % 4])
    one_level.smooth()

    pick0 = up_rows(bx + 2 * SIDE, window, SIDE // 2)
    ups0 = [up_lanes(i, LANES) for i in (0, 2)]
    fine_sent(1)
    fine_recv(1)
    grown0 = {}
    for zi in range(2 * DEEP + bz):
        rel = zi - DEEP
        key = rel // 4
        if key not in grown0:
            grown0[key] = dot(pick0, u1[PAD + n * tiles_own + key])
        side = (rel % 4) // 2
        if (key, side) not in grown0:
            grown0[(key, side)] = dot(grown0[key], ups0[side])
        p0[2, zi] = u0r[zi] + grown0[(key, side)]
    zero_level.smooth()
    for z in range(bz):
        pressure[:, z, :] = p0[2, DEEP + z, SIDE:SIDE + bx, :]
        residual[:, z, :] = zero_level.defect(DEEP + z)[SIDE:SIDE + bx]

    mid_sent(0)
    mid_sent(1)
    each_top(lambda step: top(0, step).wait_send())
    each_top(lambda step: top(1, step).wait_send())


def local(wide, narrow, rhs, coefficient, guess):
    bx, bz, by = rhs.shape
    hx = bx // 2
    z0 = bz + 2 * DEEP
    x0 = bx + 2 * SIDE
    t1 = narrow * bz // 4
    x1 = hx + 2 * SIDE
    t2 = t1 // 4
    x2 = wide * bx // 4
    x3 = x2 // 2
    vmem = lambda *shape: pltpu.VMEM(shape, jnp.float32)
    dma = lambda *shape: pltpu.SemaphoreType.DMA(shape)
    out = jax.ShapeDtypeStruct(rhs.shape, jnp.float32)
    return pl.pallas_call(
        functools.partial(kernel, wide, narrow),
        out_shape=(out, out),
        in_specs=[pl.BlockSpec(memory_space=pltpu.VMEM)] * 3,
        out_specs=[pl.BlockSpec(memory_space=pltpu.VMEM)] * 2,
        scratch_shapes=[
            vmem(3, z0, x0, by), vmem(z0, x0, by), vmem(6, z0, x0, by),
            vmem(2, t1, x1, LANES), vmem(t1, x1, LANES), vmem(t1 + 2 * PAD, x1, LANES), vmem(6, t1, x1, LANES),
            vmem(2, t2, x2, LANES), vmem(2, t2 * hx // 2, LANES), vmem(2, wide, t2 * hx // 2, LANES),
            vmem(t2, x2, LANES), vmem(6, t2, x2, LANES),
            vmem(2, 1, x3, LANES), vmem(6, 1, x3, LANES),
            dma(2, 9), dma(2, 9), dma(3, 3, narrow), dma(3, 3, narrow), dma(2, wide), dma(2, wide),
        ],
        compiler_params=pltpu.CompilerParams(collective_id=0, has_side_effects=True, vmem_limit_bytes=48 * 2**20),
    )(rhs, coefficient, guess)


def solution(mesh):
    spec = P("wide", "narrow", None)
    return jax.shard_map(
        functools.partial(local, mesh.shape["wide"], mesh.shape["narrow"]),
        mesh=mesh,
        in_specs=(spec, spec, spec),
        out_specs=(spec, spec),
        check_vma=False,
    )
```

```python
import functools

import jax
import jax.numpy as jnp
from jax import lax
from jax.experimental import pallas as pl
from jax.experimental.pallas import tpu as pltpu
from jax.sharding import PartitionSpec as P

ITERS = 20
LANES = 128
DEEP = 5
SIDE = 8
PAD = 2
MESH = pl.DeviceIdType.MESH


def dot(a, b):
    return lax.dot_general(
        a, b, (((1,), (0,)), ((), ())), precision=lax.Precision.HIGHEST, preferred_element_type=jnp.float32
    )


def iota(shape, dim):
    return lax.broadcasted_iota(jnp.int32, shape, dim)


def one(cond):
    return jnp.where(cond, 1.0, 0.0).astype(jnp.float32)


def coarse_lane(lane, part, ny):
    shift = ny.bit_length() - 1
    z = part * (LANES // ny) + (lane >> shift)
    return (z >> 1) * (ny // 2) + ((lane & (ny - 1)) >> 1)


def down_lanes(part, ny):
    shape = (LANES, LANES)
    return one(iota(shape, 1) == coarse_lane(iota(shape, 0), part, ny))


def up_lanes(part, ny):
    shape = (LANES, LANES)
    return one(iota(shape, 0) == coarse_lane(iota(shape, 1), part, ny))


def down_rows(rows):
    shape = (rows // 2, rows)
    return one(iota(shape, 0) == (iota(shape, 1) >> 1))


def up_rows(rows, coarse, first):
    shape = (rows, coarse)
    return one(iota(shape, 1) == (iota(shape, 0) >> 1) + first)


class Level:
    def __init__(self, k, f, u, wx, wy, wzp, wzm, diag, inv, ny, first, last, off=0, odd=0):
        self.k, self.f, self.u = k, f, u
        self.wx, self.wy, self.wzp, self.wzm, self.diag, self.inv = wx, wy, wzp, wzm, diag, inv
        self.ny, self.first, self.last, self.off, self.odd = ny, first, last, off, odd
        self.rows = k.shape[1]
        self.tiles = k.shape[0]

    def spin(self, v):
        if self.ny == LANES:
            return v, v
        down = pltpu.roll(v, LANES - self.ny, 1)
        return down, (down if 2 * self.ny == LANES else pltpu.roll(v, self.ny, 1))

    def above(self, here, after):
        if self.ny == LANES:
            return after[0]
        return jnp.where(iota(here[0].shape, 1) < LANES - self.ny, here[0], after[0])

    def below(self, here, before):
        if self.ny == LANES:
            return before[1]
        return jnp.where(iota(here[0].shape, 1) >= self.ny, here[1], before[1])

    def operator(self):
        shape = (self.rows, LANES)
        row = iota(shape, 0)
        y = iota(shape, 1) & (self.ny - 1)
        zero = jnp.zeros(shape, jnp.float32)
        for t in range(self.first, self.last):
            k = self.k[t]
            spun = self.spin(k)
            after = self.spin(self.k[t + 1] if t + 1 < self.tiles else zero)
            before = self.spin(self.k[t - 1] if t > 0 else zero)
            xp = jnp.where(row == self.rows - 1, 0.0, pltpu.roll(k, self.rows - 1, 0))
            xm = jnp.where(row == 0, 0.0, pltpu.roll(k, 1, 0))
            yp = jnp.where(y == self.ny - 1, 0.0, pltpu.roll(k, LANES - 1, 1))
            ym = jnp.where(y == 0, 0.0, pltpu.roll(k, 1, 1))
            zp = self.above(spun, after)
            zm = self.below(spun, before)
            diag = 3.0 * k + 0.5 * (xp + xm + zp + zm + yp + ym)
            diag = jnp.where(diag > 0.0, diag, 1.0)
            live = k > 0.0

            def face(other):
                return jnp.where(live & (other > 0.0), 0.5 * (k + other), 0.0)

            self.wx[t] = face(xp)
            self.wy[t] = face(yp)
            self.wzp[t] = face(zp)
            self.wzm[t] = face(zm)
            self.diag[t] = diag
            self.inv[t] = 1.0 / diag

    def beside(self, t, here, spun, after, before):
        wx = self.wx[t]
        wy = self.wy[t]
        total = self.wzp[t] * self.above(spun, after) + self.wzm[t] * self.below(spun, before)
        total = total + (wx * pltpu.roll(here, self.rows - 1, 0) + pltpu.roll(wx * here, 1, 0))
        return total + (wy * pltpu.roll(here, LANES - 1, 1) + pltpu.roll(wy * here, 1, 1))

    def sides(self, first, last):
        here = self.u[first + self.off]
        spun = self.spin(here)
        before = self.spin(self.u[first - 1 + self.off]) if first > 0 else spun
        for t in range(first, last):
            if t + 1 < self.tiles:
                later = self.u[t + 1 + self.off]
                after = self.spin(later)
            else:
                later, after = here, spun
            yield t, here, spun, after, before
            here, before, spun = later, spun, after

    def half_sweep(self, step, first, last):
        shape = (self.rows, LANES)
        shift = self.ny.bit_length() - 1
        lane = iota(shape, 1)
        place = iota(shape, 0) + (lane >> shift) + (lane & (self.ny - 1)) + self.odd + step
        even = (place & 1) == 0
        other = (place & 1) == 1
        for t, here, spun, after, before in self.sides(first, last):
            fresh = (self.f[t] + self.beside(t, here, spun, after, before)) * self.inv[t]
            mask = other if (self.ny == LANES and t % 2 == 1) else even
            self.u[t + self.off] = jnp.where(mask, fresh, here)

    def smooth(self):
        if self.ny == LANES:
            for step in range(4):
                self.half_sweep(step, self.first + step, self.last - step)
        else:
            @pl.loop(0, 4)
            def _(step):
                self.half_sweep(step, self.first, self.last)

    def defects(self, first, last):
        return [
            self.f[t] - (self.diag[t] * here - self.beside(t, here, spun, after, before))
            for t, here, spun, after, before in self.sides(first, last)
        ]


def kernel(wide, narrow, rhs, cond, guess, pressure, residual, *scratch):
    (ins, p0, u0r, op0, a1, u1r, u1, op1, a2, own2, g2, u2, op2, a3, op3,
     in_sem, send0, recv0, send1, recv1, send2, recv2) = scratch
    w = lax.axis_index("wide")
    n = lax.axis_index("narrow")
    bx, bz, _ = rhs.shape
    hx, hz = bx // 2, bz // 2
    own_z = pl.ds(DEEP, bz)
    own_x = pl.ds(SIDE, bx)
    tiles_own = hz // 2
    f32 = jnp.float32

    loads = [pltpu.make_async_copy(ref, ins.at[i], in_sem.at[i]) for i, ref in enumerate((cond, rhs, guess))]
    for load in loads:
        load.start()

    for ref in (p0, u0r, a1, u1r):
        ref[...] = jnp.zeros(ref.shape, f32)
    u1[...] = jnp.zeros(u1.shape, f32)

    def valid(dw):
        return (w + dw >= 0) & (w + dw < wide)

    def when(cond_, body):
        if cond_ is True:
            body()
        else:
            pl.when(cond_)(body)

    barrier = pltpu.get_barrier_semaphore()

    def greet(dev):
        pl.semaphore_signal(barrier, inc=1, device_id=dev, device_id_type=MESH)

    for j in range(1, narrow):
        greet((w, lax.rem(n + j, narrow)))
    for dw in (-1, 1):
        @pl.when(valid(dw))
        def _(dw=dw):
            for j in range(narrow):
                greet((w + dw, lax.rem(n + j, narrow)))

    @pl.loop(0, wide)
    def _(other):
        @pl.when((other < w - 1) | (other > w + 1))
        def _():
            greet((other, n))

    for i in range(3):
        loads[i].wait()
        for z in range(bz):
            p0[i, DEEP + z, SIDE:SIDE + bx, :] = ins[i, :, z, :]

    half = down_rows(bx)
    lanes0 = [down_lanes(i, LANES) for i in (0, 2)]

    def to_level_1(index, slices, factor):
        for tt in range(tiles_own):
            four = [slices[4 * tt + i] for i in range(4)]
            spread = dot(four[0] + four[1], lanes0[0]) + dot(four[2] + four[3], lanes0[1])
            a1[index, n * tiles_own + tt, SIDE:SIDE + hx, :] = factor * dot(half, spread)

    to_level_1(0, [p0[0, DEEP + z, SIDE:SIDE + bx, :] for z in range(bz)], 0.125)

    near = jnp.where(w > 0, 1, 0) + jnp.where(w < wide - 1, 1, 0)
    pl.semaphore_wait(barrier, (wide - 1 - near) + near * narrow + narrow - 1)

    zs = {1: (DEEP + bz - DEEP, 0, DEEP), -1: (DEEP, DEEP + bz, DEEP), 0: (DEEP, DEEP, bz)}
    xs = {1: (SIDE + bx - SIDE, 0, SIDE), -1: (SIDE, SIDE + bx, SIDE), 0: (SIDE, SIDE, bx)}
    around = [(dw, dn) for dw in (-1, 0, 1) for dn in (-1, 0, 1) if (dw, dn) != (0, 0)]

    def has(dw, dn):
        good = None
        if dw:
            good = valid(dw)
        if dn:
            zgood = (n + dn >= 0) & (n + dn < narrow)
            good = zgood if good is None else good & zgood
        return good

    def fine(which, dw, dn):
        src_z, dst_z, len_z = zs[dn]
        src_x, dst_x, len_x = xs[dw]
        ref = (p0.at[0], p0.at[pl.ds(1, 2)], u0r)[which]
        lead = (slice(None),) if which == 1 else ()
        src = ref.at[lead + (pl.ds(src_z, len_z), pl.ds(src_x, len_x))]
        dst = ref.at[lead + (pl.ds(dst_z, len_z), pl.ds(dst_x, len_x))]
        mine = (dw + 1) * 3 + dn + 1
        theirs = (1 - dw) * 3 + 1 - dn
        return pltpu.make_async_remote_copy(
            src_ref=src, dst_ref=dst, send_sem=send0.at[which, mine], recv_sem=recv0.at[which, theirs],
            device_id=(w + dw, n + dn), device_id_type=MESH)

    def fine_in(which, dw, dn):
        _, dst_z, len_z = zs[-dn]
        _, dst_x, len_x = xs[-dw]
        ref = (p0.at[0], p0.at[pl.ds(1, 2)], u0r)[which]
        lead = (slice(None),) if which == 1 else ()
        dst = ref.at[lead + (pl.ds(dst_z, len_z), pl.ds(dst_x, len_x))]
        mine = (dw + 1) * 3 + dn + 1
        return pltpu.make_async_remote_copy(
            src_ref=dst, dst_ref=dst, send_sem=send0.at[which, mine], recv_sem=recv0.at[which, mine],
            device_id=(w + dw, n + dn), device_id_type=MESH)

    def fine_start(which):
        for dw, dn in around:
            pl.when(has(dw, dn))(lambda dw=dw, dn=dn: fine(which, dw, dn).start())

    def fine_recv(which):
        for dw, dn in around:
            pl.when(has(dw, dn))(lambda dw=dw, dn=dn: fine_in(which, dw, dn).wait_recv())

    def fine_sent(which):
        for dw, dn in around:
            pl.when(has(dw, dn))(lambda dw=dw, dn=dn: fine(which, dw, dn).wait_send())

    mid = [(dw, j) for dw in (0, -1, 1) for j in range(narrow) if (dw, j) != (0, 0)]

    def mid_ref(which):
        return u1r if which == 2 else a1.at[which]

    def middle(which, dw, j):
        ref = mid_ref(which)
        tile = pl.ds(n * tiles_own, tiles_own)
        return pltpu.make_async_remote_copy(
            src_ref=ref.at[tile, pl.ds(SIDE, hx)], dst_ref=ref.at[tile, pl.ds(SIDE - dw * hx, hx)],
            send_sem=send1.at[which, dw + 1, j], recv_sem=recv1.at[which, 1 - dw, j],
            device_id=(w + dw, lax.rem(n + j, narrow)), device_id_type=MESH)

    def middle_in(which, dw, j):
        ref = mid_ref(which)
        src = lax.rem(n + narrow - j, narrow)
        dst = ref.at[pl.ds(src * tiles_own, tiles_own), pl.ds(SIDE + dw * hx, hx)]
        return pltpu.make_async_remote_copy(
            src_ref=dst, dst_ref=dst, send_sem=send1.at[which, dw + 1, j], recv_sem=recv1.at[which, dw + 1, j],
            device_id=(w + dw, src), device_id_type=MESH)

    def each_mid(fun):
        for dw, j in mid:
            if dw == 0:
                fun(dw, j)
            else:
                pl.when(valid(dw))(lambda dw=dw, j=j: fun(dw, j))

    def mid_start(which):
        each_mid(lambda dw, j: middle(which, dw, j).start())

    def mid_recv(which):
        each_mid(lambda dw, j: middle_in(which, dw, j).wait_recv())

    def mid_sent(which):
        each_mid(lambda dw, j: middle(which, dw, j).wait_send())

    def top(which, step):
        other = lax.rem(w + step, wide)
        return pltpu.make_async_remote_copy(
            src_ref=own2.at[which], dst_ref=g2.at[which, w], send_sem=send2.at[which, step],
            recv_sem=recv2.at[which, step], device_id=(other, n), device_id_type=MESH)

    def top_in(which, step):
        src = lax.rem(w + wide - step, wide)
        return pltpu.make_async_remote_copy(
            src_ref=own2.at[which], dst_ref=g2.at[which, src], send_sem=send2.at[which, step],
            recv_sem=recv2.at[which, step], device_id=(src, n), device_id_type=MESH)

    def each_top(fun):
        @pl.loop(1, wide)
        def _(step):
            fun(step)

    fine_start(0)
    fine_start(1)
    fine_recv(0)

    names = range(6)
    ny = LANES
    zero_level = Level(p0.at[0], p0.at[1], p0.at[2], *[op0.at[i] for i in names], LANES, 1, 2 * DEEP + bz - 1, odd=1)
    zero_level.operator()
    fine_recv(1)
    mid_start(0)
    fine_sent(0)
    fine_sent(1)
    zero_level.smooth()
    to_level_1(1, [v[SIDE:SIDE + bx] for v in zero_level.defects(DEEP, DEEP + bz)], 0.5)
    mid_start(1)
    u0r[own_z, own_x, :] = p0[2, own_z, own_x, :]
    fine_start(2)

    ny1, ny2, ny3 = LANES // 2, LANES // 4, LANES // 8
    mid_recv(0)
    one_level = Level(a1.at[0], a1.at[1], u1, *[op1.at[i] for i in names], ny1, 0, a1.shape[1], off=PAD)
    rows2 = hx // 2
    lanes1 = [down_lanes(i, ny1) for i in range(4)]
    tiles2 = a1.shape[1] // 4

    def to_level_2(which, tiles, factor):
        shape = (tiles2 * rows2, hx)
        pack = None
        for big in range(tiles2):
            spread = dot(tiles[4 * big], lanes1[0])
            for i in range(1, 4):
                spread = spread + dot(tiles[4 * big + i], lanes1[i])
            place = one(iota(shape, 0) == (iota(shape, 1) >> 1) + big * rows2)
            part = dot(place, spread)
            pack = part if pack is None else pack + part
        pack = factor * pack
        own2[which] = pack
        g2[which, w] = pack

    to_level_2(0, [a1[0, t, SIDE:SIDE + hx, :] for t in range(a1.shape[1])], 0.125)
    each_top(lambda step: top(0, step).start())
    one_level.operator()
    mid_recv(1)
    one_level.smooth()
    to_level_2(1, [v[SIDE:SIDE + hx] for v in one_level.defects(0, a1.shape[1])], 0.5)
    each_top(lambda step: top(1, step).start())
    u1r[pl.ds(n * tiles_own, tiles_own), SIDE:SIDE + hx, :] = u1[pl.ds(PAD + n * tiles_own, tiles_own), SIDE:SIDE + hx, :]
    mid_start(2)

    def unpack(which):
        for other in range(wide):
            for t in range(tiles2):
                a2[which, t, other * rows2:(other + 1) * rows2, :] = g2[which, other, t * rows2:(t + 1) * rows2, :]

    each_top(lambda step: top_in(0, step).wait_recv())
    unpack(0)
    two_level = Level(a2.at[0], a2.at[1], u2, *[op2.at[i] for i in names], ny2, 0, tiles2)
    two_level.operator()
    all2, all3 = a2.shape[2], a3.shape[2]
    half2 = down_rows(all2)
    lanes2 = [down_lanes(i, ny2) for i in range(tiles2)]

    def to_level_3(tiles, factor):
        spread = dot(tiles[0], lanes2[0])
        for i in range(1, tiles2):
            spread = spread + dot(tiles[i], lanes2[i])
        return factor * dot(half2, spread)

    a3[0, 0] = to_level_3([a2[0, t] for t in range(tiles2)], 0.125)
    last = Level(a3.at[0], a3.at[1], a3.at[1], *[op3.at[i] for i in names], ny3, 0, 1)
    last.operator()
    each_top(lambda step: top_in(1, step).wait_recv())
    unpack(1)
    u2[...] = jnp.zeros(u2.shape, f32)
    two_level.smooth()
    source = to_level_3(two_level.defects(0, tiles2), 0.5)

    def image(v):
        spun = last.spin(v)
        return last.diag[0] * v - last.beside(0, v, spun, spun, spun)

    def total(v):
        return jnp.sum(jnp.sum(v, axis=0, keepdims=True), axis=1, keepdims=True)

    def advance(step, carry):
        answer, remain, wave, search, moved, twice, norm, rate = carry
        norm_next = total(remain * remain)
        cross = total(wave * remain)
        ahead = image(wave)
        beta = jnp.where(step == 0, 0.0, norm_next / norm)
        below = cross - beta * (norm_next * rate)
        alpha = norm_next / below
        rate = below / norm_next
        twice = ahead + beta * twice
        moved = wave + beta * moved
        search = remain + beta * search
        answer = answer + alpha * search
        remain = remain - alpha * moved
        wave = wave - alpha * twice
        return answer, remain, wave, search, moved, twice, norm_next, rate

    nothing = jnp.zeros_like(source)
    unit = jnp.ones((1, 1), f32)
    carry = (nothing, source, image(source), nothing, nothing, nothing, unit, unit)
    solved = lax.fori_loop(0, ITERS, advance, carry)[0]

    wider = dot(up_rows(all2, all3, 0), solved)
    for t in range(tiles2):
        u2[t] = u2[t] + dot(wider, up_lanes(t, ny2))
    two_level.smooth()

    window = a1.shape[2]
    pick = up_rows(window, all2, w * rows2 - SIDE // 2)
    grown = [dot(pick, u2[t]) for t in range(tiles2)]
    mid_sent(2)
    mid_recv(2)
    ups1 = [up_lanes(i, ny1) for i in range(4)]
    for t in range(a1.shape[1]):
        u1[PAD + t] = u1r[t] + dot(grown[t // 4], ups1[t % 4])
    one_level.smooth()

    pick0 = up_rows(bx + 2 * SIDE, window, SIDE // 2)
    ups0 = [up_lanes(i, LANES) for i in (0, 2)]
    fine_sent(2)
    fine_recv(2)
    grown0 = {}
    for zi in range(2 * DEEP + bz):
        rel = zi - DEEP
        key = rel // 4
        if key not in grown0:
            grown0[key] = dot(pick0, u1[PAD + n * tiles_own + key])
        side = (rel % 4) // 2
        if (key, side) not in grown0:
            grown0[(key, side)] = dot(grown0[key], ups0[side])
        p0[2, zi] = u0r[zi] + grown0[(key, side)]
    zero_level.smooth()
    for z, left in enumerate(zero_level.defects(DEEP, DEEP + bz)):
        pressure[:, z, :] = p0[2, DEEP + z, SIDE:SIDE + bx, :]
        residual[:, z, :] = left[SIDE:SIDE + bx]

    mid_sent(0)
    mid_sent(1)
    each_top(lambda step: top(0, step).wait_send())
    each_top(lambda step: top(1, step).wait_send())


def local(wide, narrow, rhs, coefficient, guess):
    bx, bz, by = rhs.shape
    hx = bx // 2
    z0 = bz + 2 * DEEP
    x0 = bx + 2 * SIDE
    t1 = narrow * bz // 4
    x1 = hx + 2 * SIDE
    t2 = t1 // 4
    x2 = wide * bx // 4
    x3 = x2 // 2
    vmem = lambda *shape: pltpu.VMEM(shape, jnp.float32)
    dma = lambda *shape: pltpu.SemaphoreType.DMA(shape)
    out = jax.ShapeDtypeStruct(rhs.shape, jnp.float32)
    return pl.pallas_call(
        functools.partial(kernel, wide, narrow),
        out_shape=(out, out),
        in_specs=[pl.BlockSpec(memory_space=pl.ANY)] * 3,
        out_specs=[pl.BlockSpec(memory_space=pltpu.VMEM)] * 2,
        scratch_shapes=[
            vmem(3, bx, bz, by), vmem(3, z0, x0, by), vmem(z0, x0, by), vmem(6, z0, x0, by),
            vmem(2, t1, x1, LANES), vmem(t1, x1, LANES), vmem(t1 + 2 * PAD, x1, LANES), vmem(6, t1, x1, LANES),
            vmem(2, t2, x2, LANES), vmem(2, t2 * hx // 2, LANES), vmem(2, wide, t2 * hx // 2, LANES),
            vmem(t2, x2, LANES), vmem(6, t2, x2, LANES),
            vmem(2, 1, x3, LANES), vmem(6, 1, x3, LANES),
            dma(3), dma(3, 9), dma(3, 9), dma(3, 3, narrow), dma(3, 3, narrow), dma(2, wide), dma(2, wide),
        ],
        compiler_params=pltpu.CompilerParams(collective_id=0, has_side_effects=True, vmem_limit_bytes=48 * 2**20),
    )(rhs, coefficient, guess)


def solution(mesh):
    spec = P("wide", "narrow", None)
    return jax.shard_map(
        functools.partial(local, mesh.shape["wide"], mesh.shape["narrow"]),
        mesh=mesh,
        in_specs=(spec, spec, spec),
        out_specs=(spec, spec),
        check_vma=False,
    )
```

```python
import functools

import jax
import jax.numpy as jnp
from jax import lax
from jax.experimental import pallas as pl
from jax.experimental.pallas import tpu as pltpu
from jax.sharding import PartitionSpec as P

ITERS = 20
LANES = 128
DEEP = 5
SIDE = 8
PAD = 2
MESH = pl.DeviceIdType.MESH


def dot(a, b):
    return lax.dot_general(a, b, (((1,), (0,)), ((), ())), preferred_element_type=jnp.float32)


def split(a):
    high = a.astype(jnp.bfloat16).astype(jnp.float32)
    rest = a - high
    mid = rest.astype(jnp.bfloat16).astype(jnp.float32)
    return jnp.concatenate([high, mid, rest - mid], axis=0).astype(jnp.bfloat16)


def map_lanes(a, matrix):
    rows = a.shape[0]
    out = dot(split(a), matrix)
    return out[:rows] + (out[rows:2 * rows] + out[2 * rows:])


def map_rows(matrix, a):
    return dot(jnp.concatenate([matrix, matrix, matrix], axis=1).astype(jnp.bfloat16), split(a))


def beside_each(parts):
    return jnp.concatenate(parts, axis=1)


def stacked(parts):
    return jnp.concatenate(parts, axis=0)


def iota(shape, dim):
    return lax.broadcasted_iota(jnp.int32, shape, dim)


def one(cond):
    return jnp.where(cond, 1.0, 0.0).astype(jnp.float32)


def coarse_lane(lane, part, ny):
    shift = ny.bit_length() - 1
    z = part * (LANES // ny) + (lane >> shift)
    return (z >> 1) * (ny // 2) + ((lane & (ny - 1)) >> 1)


def down_lanes(part, ny):
    shape = (LANES, LANES)
    return one(iota(shape, 1) == coarse_lane(iota(shape, 0), part, ny))


def up_lanes(part, ny):
    shape = (LANES, LANES)
    return one(iota(shape, 0) == coarse_lane(iota(shape, 1), part, ny))


def down_rows(rows):
    shape = (rows // 2, rows)
    return one(iota(shape, 0) == (iota(shape, 1) >> 1))


def up_rows(rows, coarse, first):
    shape = (rows, coarse)
    return one(iota(shape, 1) == (iota(shape, 0) >> 1) + first)


class Level:
    def __init__(self, k, f, u, wx, wy, wzp, wzm, diag, inv, ny, first, last, off=0, odd=0):
        self.k, self.f, self.u = k, f, u
        self.wx, self.wy, self.wzp, self.wzm, self.diag, self.inv = wx, wy, wzp, wzm, diag, inv
        self.ny, self.first, self.last, self.off, self.odd = ny, first, last, off, odd
        self.rows = k.shape[1]
        self.tiles = k.shape[0]

    def spin(self, v):
        if self.ny == LANES:
            return v, v
        down = pltpu.roll(v, LANES - self.ny, 1)
        return down, (down if 2 * self.ny == LANES else pltpu.roll(v, self.ny, 1))

    def above(self, here, after):
        if self.ny == LANES:
            return after[0]
        return jnp.where(iota(here[0].shape, 1) < LANES - self.ny, here[0], after[0])

    def below(self, here, before):
        if self.ny == LANES:
            return before[1]
        return jnp.where(iota(here[0].shape, 1) >= self.ny, here[1], before[1])

    def operator(self):
        shape = (self.rows, LANES)
        row = iota(shape, 0)
        y = iota(shape, 1) & (self.ny - 1)
        zero = jnp.zeros(shape, jnp.float32)
        for t in range(self.first, self.last):
            k = self.k[t]
            spun = self.spin(k)
            after = self.spin(self.k[t + 1] if t + 1 < self.tiles else zero)
            before = self.spin(self.k[t - 1] if t > 0 else zero)
            xp = jnp.where(row == self.rows - 1, 0.0, pltpu.roll(k, self.rows - 1, 0))
            xm = jnp.where(row == 0, 0.0, pltpu.roll(k, 1, 0))
            yp = jnp.where(y == self.ny - 1, 0.0, pltpu.roll(k, LANES - 1, 1))
            ym = jnp.where(y == 0, 0.0, pltpu.roll(k, 1, 1))
            zp = self.above(spun, after)
            zm = self.below(spun, before)
            diag = 3.0 * k + 0.5 * (xp + xm + zp + zm + yp + ym)
            diag = jnp.where(diag > 0.0, diag, 1.0)
            live = k > 0.0

            def face(other):
                return jnp.where(live & (other > 0.0), 0.5 * (k + other), 0.0)

            self.wx[t] = face(xp)
            self.wy[t] = face(yp)
            self.wzp[t] = face(zp)
            self.wzm[t] = face(zm)
            self.diag[t] = diag
            self.inv[t] = 1.0 / diag

    def beside(self, t, here, spun, after, before):
        wx = self.wx[t]
        wy = self.wy[t]
        total = self.wzp[t] * self.above(spun, after) + self.wzm[t] * self.below(spun, before)
        total = total + (wx * pltpu.roll(here, self.rows - 1, 0) + pltpu.roll(wx * here, 1, 0))
        return total + (wy * pltpu.roll(here, LANES - 1, 1) + pltpu.roll(wy * here, 1, 1))

    def sides(self, first, last):
        here = self.u[first + self.off]
        spun = self.spin(here)
        before = self.spin(self.u[first - 1 + self.off]) if first > 0 else spun
        for t in range(first, last):
            if t + 1 < self.tiles:
                later = self.u[t + 1 + self.off]
                after = self.spin(later)
            else:
                later, after = here, spun
            yield t, here, spun, after, before
            here, before, spun = later, spun, after

    def half_sweep(self, step, first, last):
        shape = (self.rows, LANES)
        shift = self.ny.bit_length() - 1
        lane = iota(shape, 1)
        place = iota(shape, 0) + (lane >> shift) + (lane & (self.ny - 1)) + self.odd + step
        even = (place & 1) == 0
        other = (place & 1) == 1
        for t, here, spun, after, before in self.sides(first, last):
            fresh = (self.f[t] + self.beside(t, here, spun, after, before)) * self.inv[t]
            mask = other if (self.ny == LANES and t % 2 == 1) else even
            self.u[t + self.off] = jnp.where(mask, fresh, here)

    def smooth(self):
        if self.ny == LANES:
            for step in range(4):
                self.half_sweep(step, self.first + step, self.last - step)
        else:
            @pl.loop(0, 4)
            def _(step):
                self.half_sweep(step, self.first, self.last)

    def defects(self, first, last):
        return [
            self.f[t] - (self.diag[t] * here - self.beside(t, here, spun, after, before))
            for t, here, spun, after, before in self.sides(first, last)
        ]


def kernel(wide, narrow, rhs, cond, guess, pressure, residual, *scratch):
    (ins, p0, u0r, op0, a1, u1r, u1, op1, a2, own2, g2, u2, op2, a3, op3, down0, up0, down1, up1, down2, up2,
     in_sem, send0, recv0, send1, recv1, send2, recv2) = scratch
    w = lax.axis_index("wide")
    n = lax.axis_index("narrow")
    bx, bz, _ = rhs.shape
    hx, hz = bx // 2, bz // 2
    own_z = pl.ds(DEEP, bz)
    own_x = pl.ds(SIDE, bx)
    tiles_own = hz // 2
    f32 = jnp.float32

    loads = [pltpu.make_async_copy(ref, ins.at[i], in_sem.at[i]) for i, ref in enumerate((cond, rhs, guess))]
    for load in loads:
        load.start()

    for ref in (p0, u0r, a1, u1r):
        ref[...] = jnp.zeros(ref.shape, f32)
    u1[...] = jnp.zeros(u1.shape, f32)

    def valid(dw):
        return (w + dw >= 0) & (w + dw < wide)

    def when(cond_, body):
        if cond_ is True:
            body()
        else:
            pl.when(cond_)(body)

    barrier = pltpu.get_barrier_semaphore()

    def greet(dev):
        pl.semaphore_signal(barrier, inc=1, device_id=dev, device_id_type=MESH)

    for j in range(1, narrow):
        greet((w, lax.rem(n + j, narrow)))
    for dw in (-1, 1):
        @pl.when(valid(dw))
        def _(dw=dw):
            for j in range(narrow):
                greet((w + dw, lax.rem(n + j, narrow)))

    @pl.loop(0, wide)
    def _(other):
        @pl.when((other < w - 1) | (other > w + 1))
        def _():
            greet((other, n))

    for i in range(3):
        loads[i].wait()
        for z in range(bz):
            p0[i, DEEP + z, SIDE:SIDE + bx, :] = ins[i, :, z, :]

    def to_level_1(index, slices, factor):
        pairs = beside_each([slices[2 * i] + slices[2 * i + 1] for i in range(hz)])
        thin = map_rows(down_rows(bx), pairs)
        flat = stacked([thin[:, 2 * LANES * tt:2 * LANES * (tt + 1)] for tt in range(tiles_own)])
        done = factor * map_lanes(flat, down0[...])
        for tt in range(tiles_own):
            a1[index, n * tiles_own + tt, SIDE:SIDE + hx, :] = done[hx * tt:hx * (tt + 1)]

    near = jnp.where(w > 0, 1, 0) + jnp.where(w < wide - 1, 1, 0)
    pl.semaphore_wait(barrier, (wide - 1 - near) + near * narrow + narrow - 1)

    zs = {1: (DEEP + bz - DEEP, 0, DEEP), -1: (DEEP, DEEP + bz, DEEP), 0: (DEEP, DEEP, bz)}
    xs = {1: (SIDE + bx - SIDE, 0, SIDE), -1: (SIDE, SIDE + bx, SIDE), 0: (SIDE, SIDE, bx)}
    around = [(dw, dn) for dw in (-1, 0, 1) for dn in (-1, 0, 1) if (dw, dn) != (0, 0)]

    def has(dw, dn):
        good = None
        if dw:
            good = valid(dw)
        if dn:
            zgood = (n + dn >= 0) & (n + dn < narrow)
            good = zgood if good is None else good & zgood
        return good

    def fine(which, dw, dn):
        src_z, dst_z, len_z = zs[dn]
        src_x, dst_x, len_x = xs[dw]
        ref = (p0.at[0], p0.at[pl.ds(1, 2)], u0r)[which]
        lead = (slice(None),) if which == 1 else ()
        src = ref.at[lead + (pl.ds(src_z, len_z), pl.ds(src_x, len_x))]
        dst = ref.at[lead + (pl.ds(dst_z, len_z), pl.ds(dst_x, len_x))]
        mine = (dw + 1) * 3 + dn + 1
        theirs = (1 - dw) * 3 + 1 - dn
        return pltpu.make_async_remote_copy(
            src_ref=src, dst_ref=dst, send_sem=send0.at[which, mine], recv_sem=recv0.at[which, theirs],
            device_id=(w + dw, n + dn), device_id_type=MESH)

    def fine_in(which, dw, dn):
        _, dst_z, len_z = zs[-dn]
        _, dst_x, len_x = xs[-dw]
        ref = (p0.at[0], p0.at[pl.ds(1, 2)], u0r)[which]
        lead = (slice(None),) if which == 1 else ()
        dst = ref.at[lead + (pl.ds(dst_z, len_z), pl.ds(dst_x, len_x))]
        mine = (dw + 1) * 3 + dn + 1
        return pltpu.make_async_remote_copy(
            src_ref=dst, dst_ref=dst, send_sem=send0.at[which, mine], recv_sem=recv0.at[which, mine],
            device_id=(w + dw, n + dn), device_id_type=MESH)

    def fine_start(which):
        for dw, dn in around:
            pl.when(has(dw, dn))(lambda dw=dw, dn=dn: fine(which, dw, dn).start())

    def fine_recv(which):
        for dw, dn in around:
            pl.when(has(dw, dn))(lambda dw=dw, dn=dn: fine_in(which, dw, dn).wait_recv())

    def fine_sent(which):
        for dw, dn in around:
            pl.when(has(dw, dn))(lambda dw=dw, dn=dn: fine(which, dw, dn).wait_send())

    mid = [(dw, j) for dw in (0, -1, 1) for j in range(narrow) if (dw, j) != (0, 0)]

    def mid_ref(which):
        return u1r if which == 2 else a1.at[which]

    def middle(which, dw, j):
        ref = mid_ref(which)
        tile = pl.ds(n * tiles_own, tiles_own)
        return pltpu.make_async_remote_copy(
            src_ref=ref.at[tile, pl.ds(SIDE, hx)], dst_ref=ref.at[tile, pl.ds(SIDE - dw * hx, hx)],
            send_sem=send1.at[which, dw + 1, j], recv_sem=recv1.at[which, 1 - dw, j],
            device_id=(w + dw, lax.rem(n + j, narrow)), device_id_type=MESH)

    def middle_in(which, dw, j):
        ref = mid_ref(which)
        src = lax.rem(n + narrow - j, narrow)
        dst = ref.at[pl.ds(src * tiles_own, tiles_own), pl.ds(SIDE + dw * hx, hx)]
        return pltpu.make_async_remote_copy(
            src_ref=dst, dst_ref=dst, send_sem=send1.at[which, dw + 1, j], recv_sem=recv1.at[which, dw + 1, j],
            device_id=(w + dw, src), device_id_type=MESH)

    def each_mid(fun):
        for dw, j in mid:
            if dw == 0:
                fun(dw, j)
            else:
                pl.when(valid(dw))(lambda dw=dw, j=j: fun(dw, j))

    def mid_start(which):
        each_mid(lambda dw, j: middle(which, dw, j).start())

    def mid_recv(which):
        each_mid(lambda dw, j: middle_in(which, dw, j).wait_recv())

    def mid_sent(which):
        each_mid(lambda dw, j: middle(which, dw, j).wait_send())

    def top(which, step):
        other = lax.rem(w + step, wide)
        return pltpu.make_async_remote_copy(
            src_ref=own2.at[which], dst_ref=g2.at[which, w], send_sem=send2.at[which, step],
            recv_sem=recv2.at[which, step], device_id=(other, n), device_id_type=MESH)

    def top_in(which, step):
        src = lax.rem(w + wide - step, wide)
        return pltpu.make_async_remote_copy(
            src_ref=own2.at[which], dst_ref=g2.at[which, src], send_sem=send2.at[which, step],
            recv_sem=recv2.at[which, step], device_id=(src, n), device_id_type=MESH)

    def each_top(fun):
        @pl.loop(1, wide)
        def _(step):
            fun(step)

    fine_start(0)
    fine_start(1)

    names = range(6)
    ny1, ny2, ny3 = LANES // 2, LANES // 4, LANES // 8
    tiles2 = a1.shape[1] // 4
    bf16 = jnp.bfloat16
    down0[...] = stacked([down_lanes(i, LANES) for i in (0, 2)]).astype(bf16)
    up0[...] = beside_each([up_lanes(i, LANES) for i in (0, 2)]).astype(bf16)
    down1[...] = stacked([down_lanes(i, ny1) for i in range(4)]).astype(bf16)
    up1[...] = beside_each([up_lanes(i, ny1) for i in range(4)]).astype(bf16)
    down2[...] = stacked([down_lanes(i, ny2) for i in range(tiles2)]).astype(bf16)
    up2[...] = beside_each([up_lanes(i, ny2) for i in range(tiles2)]).astype(bf16)
    to_level_1(0, [p0[0, DEEP + z, SIDE:SIDE + bx, :] for z in range(bz)], 0.125)
    fine_recv(0)
    zero_level = Level(p0.at[0], p0.at[1], p0.at[2], *[op0.at[i] for i in names], LANES, 1, 2 * DEEP + bz - 1, odd=1)
    zero_level.operator()
    fine_recv(1)
    mid_start(0)
    fine_sent(0)
    fine_sent(1)
    zero_level.smooth()
    to_level_1(1, [v[SIDE:SIDE + bx] for v in zero_level.defects(DEEP, DEEP + bz)], 0.5)
    mid_start(1)
    u0r[own_z, own_x, :] = p0[2, own_z, own_x, :]
    fine_start(2)

    mid_recv(0)
    one_level = Level(a1.at[0], a1.at[1], u1, *[op1.at[i] for i in names], ny1, 0, a1.shape[1], off=PAD)
    rows2 = hx // 2

    def to_level_2(which, tiles, factor):
        flat = stacked([beside_each(tiles[4 * big:4 * big + 4]) for big in range(tiles2)])
        pack = factor * map_rows(down_rows(tiles2 * hx), map_lanes(flat, down1[...]))
        own2[which] = pack
        g2[which, w] = pack

    to_level_2(0, [a1[0, t, SIDE:SIDE + hx, :] for t in range(a1.shape[1])], 0.125)
    each_top(lambda step: top(0, step).start())
    one_level.operator()
    mid_recv(1)
    one_level.smooth()
    to_level_2(1, [v[SIDE:SIDE + hx] for v in one_level.defects(0, a1.shape[1])], 0.5)
    each_top(lambda step: top(1, step).start())
    u1r[pl.ds(n * tiles_own, tiles_own), SIDE:SIDE + hx, :] = u1[pl.ds(PAD + n * tiles_own, tiles_own), SIDE:SIDE + hx, :]
    mid_start(2)

    def unpack(which):
        for other in range(wide):
            for t in range(tiles2):
                a2[which, t, other * rows2:(other + 1) * rows2, :] = g2[which, other, t * rows2:(t + 1) * rows2, :]

    each_top(lambda step: top_in(0, step).wait_recv())
    unpack(0)
    two_level = Level(a2.at[0], a2.at[1], u2, *[op2.at[i] for i in names], ny2, 0, tiles2)
    two_level.operator()
    all2, all3 = a2.shape[2], a3.shape[2]

    def to_level_3(tiles, factor):
        return factor * map_rows(down_rows(all2), map_lanes(beside_each(tiles), down2[...]))

    a3[0, 0] = to_level_3([a2[0, t] for t in range(tiles2)], 0.125)
    last = Level(a3.at[0], a3.at[1], a3.at[1], *[op3.at[i] for i in names], ny3, 0, 1)
    last.operator()
    each_top(lambda step: top_in(1, step).wait_recv())
    unpack(1)
    u2[...] = jnp.zeros(u2.shape, f32)
    two_level.smooth()
    source = to_level_3(two_level.defects(0, tiles2), 0.5)

    def image(v):
        spun = last.spin(v)
        return last.diag[0] * v - last.beside(0, v, spun, spun, spun)

    def total(v):
        return jnp.sum(jnp.sum(v, axis=0, keepdims=True), axis=1, keepdims=True)

    def advance(step, carry):
        answer, remain, wave, search, moved, twice, norm, rate = carry
        norm_next = total(remain * remain)
        cross = total(wave * remain)
        ahead = image(wave)
        beta = jnp.where(step == 0, 0.0, norm_next / norm)
        below = cross - beta * (norm_next * rate)
        alpha = norm_next / below
        rate = below / norm_next
        twice = ahead + beta * twice
        moved = wave + beta * moved
        search = remain + beta * search
        answer = answer + alpha * search
        remain = remain - alpha * moved
        wave = wave - alpha * twice
        return answer, remain, wave, search, moved, twice, norm_next, rate

    nothing = jnp.zeros_like(source)
    unit = jnp.ones((1, 1), f32)
    carry = (nothing, source, image(source), nothing, nothing, nothing, unit, unit)
    solved = lax.fori_loop(0, ITERS, advance, carry)[0]

    wider = map_lanes(map_rows(up_rows(all2, all3, 0), solved), up2[...])
    for t in range(tiles2):
        u2[t] = u2[t] + wider[:, LANES * t:LANES * (t + 1)]
    two_level.smooth()

    window = a1.shape[2]
    pick = up_rows(window, all2, w * rows2 - SIDE // 2)
    thin = map_rows(pick, beside_each([u2[t] for t in range(tiles2)]))
    grown = map_lanes(stacked([thin[:, LANES * t:LANES * (t + 1)] for t in range(tiles2)]), up1[...])
    mid_sent(2)
    mid_recv(2)
    for t in range(a1.shape[1]):
        big, i = t // 4, t % 4
        u1[PAD + t] = u1r[t] + grown[window * big:window * (big + 1), LANES * i:LANES * (i + 1)]
    one_level.smooth()

    pick0 = up_rows(bx + 2 * SIDE, window, SIDE // 2)
    low, high = -DEEP // 4, (bz + DEEP - 1) // 4
    thin = map_rows(pick0, beside_each([u1[PAD + n * tiles_own + key] for key in range(low, high + 1)]))
    span = thin.shape[0]
    grown = map_lanes(stacked([thin[:, LANES * t:LANES * (t + 1)] for t in range(high + 1 - low)]), up0[...])
    fine_sent(2)
    fine_recv(2)
    for zi in range(2 * DEEP + bz):
        t = (zi - DEEP) // 4 - low
        side = ((zi - DEEP) % 4) // 2
        p0[2, zi] = u0r[zi] + grown[span * t:span * (t + 1), LANES * side:LANES * (side + 1)]
    zero_level.smooth()
    for z, left in enumerate(zero_level.defects(DEEP, DEEP + bz)):
        pressure[:, z, :] = p0[2, DEEP + z, SIDE:SIDE + bx, :]
        residual[:, z, :] = left[SIDE:SIDE + bx]

    mid_sent(0)
    mid_sent(1)
    each_top(lambda step: top(0, step).wait_send())
    each_top(lambda step: top(1, step).wait_send())


def local(wide, narrow, rhs, coefficient, guess):
    bx, bz, by = rhs.shape
    hx = bx // 2
    z0 = bz + 2 * DEEP
    x0 = bx + 2 * SIDE
    t1 = narrow * bz // 4
    x1 = hx + 2 * SIDE
    t2 = t1 // 4
    x2 = wide * bx // 4
    x3 = x2 // 2
    vmem = lambda *shape: pltpu.VMEM(shape, jnp.float32)
    half = lambda *shape: pltpu.VMEM(shape, jnp.bfloat16)
    dma = lambda *shape: pltpu.SemaphoreType.DMA(shape)
    out = jax.ShapeDtypeStruct(rhs.shape, jnp.float32)
    return pl.pallas_call(
        functools.partial(kernel, wide, narrow),
        out_shape=(out, out),
        in_specs=[pl.BlockSpec(memory_space=pltpu.HBM)] * 3,
        out_specs=[pl.BlockSpec(memory_space=pltpu.VMEM)] * 2,
        scratch_shapes=[
            vmem(3, bx, bz, by), vmem(3, z0, x0, by), vmem(z0, x0, by), vmem(6, z0, x0, by),
            vmem(2, t1, x1, LANES), vmem(t1, x1, LANES), vmem(t1 + 2 * PAD, x1, LANES), vmem(6, t1, x1, LANES),
            vmem(2, t2, x2, LANES), vmem(2, t2 * hx // 2, LANES), vmem(2, wide, t2 * hx // 2, LANES),
            vmem(t2, x2, LANES), vmem(6, t2, x2, LANES),
            vmem(2, 1, x3, LANES), vmem(6, 1, x3, LANES),
            half(2 * LANES, LANES), half(LANES, 2 * LANES), half(4 * LANES, LANES), half(LANES, 4 * LANES),
            half(t2 * LANES, LANES), half(LANES, t2 * LANES),
            dma(3), dma(3, 9), dma(3, 9), dma(3, 3, narrow), dma(3, 3, narrow), dma(2, wide), dma(2, wide),
        ],
        compiler_params=pltpu.CompilerParams(collective_id=0, has_side_effects=True, vmem_limit_bytes=48 * 2**20),
    )(rhs, coefficient, guess)


def solution(mesh):
    spec = P("wide", "narrow", None)
    return jax.shard_map(
        functools.partial(local, mesh.shape["wide"], mesh.shape["narrow"]),
        mesh=mesh,
        in_specs=(spec, spec, spec),
        out_specs=(spec, spec),
        check_vma=False,
    )
```

```python
import functools

import jax
import jax.numpy as jnp
from jax import lax
from jax.experimental import pallas as pl
from jax.experimental.pallas import tpu as pltpu
from jax.sharding import PartitionSpec as P

ITERS = 20
LANES = 128
DEEP = 5
SIDE = 8
PAD = 2
MESH = pl.DeviceIdType.MESH


def dot(a, b):
    return lax.dot_general(a, b, (((1,), (0,)), ((), ())), preferred_element_type=jnp.float32)


def split(a):
    high = a.astype(jnp.bfloat16).astype(jnp.float32)
    rest = a - high
    mid = rest.astype(jnp.bfloat16).astype(jnp.float32)
    return jnp.concatenate([high, mid, rest - mid], axis=0).astype(jnp.bfloat16)


def map_lanes(a, matrix):
    rows = a.shape[0]
    out = dot(split(a), matrix)
    return out[:rows] + (out[rows:2 * rows] + out[2 * rows:])


def map_rows(matrix, a):
    return dot(jnp.concatenate([matrix, matrix, matrix], axis=1).astype(jnp.bfloat16), split(a))


def beside_each(parts):
    return jnp.concatenate(parts, axis=1)


def stacked(parts):
    return jnp.concatenate(parts, axis=0)


def iota(shape, dim):
    return lax.broadcasted_iota(jnp.int32, shape, dim)


def one(cond):
    return jnp.where(cond, 1.0, 0.0).astype(jnp.float32)


def coarse_lane(lane, part, ny):
    shift = ny.bit_length() - 1
    z = part * (LANES // ny) + (lane >> shift)
    return (z >> 1) * (ny // 2) + ((lane & (ny - 1)) >> 1)


def down_lanes(part, ny):
    shape = (LANES, LANES)
    return one(iota(shape, 1) == coarse_lane(iota(shape, 0), part, ny))


def up_lanes(part, ny):
    shape = (LANES, LANES)
    return one(iota(shape, 0) == coarse_lane(iota(shape, 1), part, ny))


def down_rows(rows):
    shape = (rows // 2, rows)
    return one(iota(shape, 0) == (iota(shape, 1) >> 1))


def up_rows(rows, coarse, first):
    shape = (rows, coarse)
    return one(iota(shape, 1) == (iota(shape, 0) >> 1) + first)


class Level:
    def __init__(self, k, f, u, wx, wy, wzp, wzm, diag, inv, ny, first, last, off=0, odd=0):
        self.k, self.f, self.u = k, f, u
        self.wx, self.wy, self.wzp, self.wzm, self.diag, self.inv = wx, wy, wzp, wzm, diag, inv
        self.ny, self.first, self.last, self.off, self.odd = ny, first, last, off, odd
        self.rows = k.shape[1]
        self.tiles = k.shape[0]

    def spin(self, v):
        if self.ny == LANES:
            return v, v
        down = pltpu.roll(v, LANES - self.ny, 1)
        return down, (down if 2 * self.ny == LANES else pltpu.roll(v, self.ny, 1))

    def above(self, here, after):
        if self.ny == LANES:
            return after[0]
        return jnp.where(iota(here[0].shape, 1) < LANES - self.ny, here[0], after[0])

    def below(self, here, before):
        if self.ny == LANES:
            return before[1]
        return jnp.where(iota(here[0].shape, 1) >= self.ny, here[1], before[1])

    def operator(self):
        shape = (self.rows, LANES)
        row = iota(shape, 0)
        y = iota(shape, 1) & (self.ny - 1)
        zero = jnp.zeros(shape, jnp.float32)
        for t in range(self.first, self.last):
            k = self.k[t]
            spun = self.spin(k)
            after = self.spin(self.k[t + 1] if t + 1 < self.tiles else zero)
            before = self.spin(self.k[t - 1] if t > 0 else zero)
            xp = jnp.where(row == self.rows - 1, 0.0, pltpu.roll(k, self.rows - 1, 0))
            xm = jnp.where(row == 0, 0.0, pltpu.roll(k, 1, 0))
            yp = jnp.where(y == self.ny - 1, 0.0, pltpu.roll(k, LANES - 1, 1))
            ym = jnp.where(y == 0, 0.0, pltpu.roll(k, 1, 1))
            zp = self.above(spun, after)
            zm = self.below(spun, before)
            diag = 3.0 * k + 0.5 * (xp + xm + zp + zm + yp + ym)
            diag = jnp.where(diag > 0.0, diag, 1.0)
            live = k > 0.0

            def face(other):
                return jnp.where(live & (other > 0.0), 0.5 * (k + other), 0.0)

            self.wx[t] = face(xp)
            self.wy[t] = face(yp)
            self.wzp[t] = face(zp)
            self.wzm[t] = face(zm)
            self.diag[t] = diag
            self.inv[t] = 1.0 / diag

    def beside(self, t, here, spun, after, before):
        wx = self.wx[t]
        wy = self.wy[t]
        total = self.wzp[t] * self.above(spun, after) + self.wzm[t] * self.below(spun, before)
        total = total + (wx * pltpu.roll(here, self.rows - 1, 0) + pltpu.roll(wx * here, 1, 0))
        return total + (wy * pltpu.roll(here, LANES - 1, 1) + pltpu.roll(wy * here, 1, 1))

    def sides(self, first, last):
        here = self.u[first + self.off]
        spun = self.spin(here)
        before = self.spin(self.u[first - 1 + self.off]) if first > 0 else spun
        for t in range(first, last):
            if t + 1 < self.tiles:
                later = self.u[t + 1 + self.off]
                after = self.spin(later)
            else:
                later, after = here, spun
            yield t, here, spun, after, before
            here, before, spun = later, spun, after

    def half_sweep(self, step, first, last):
        shape = (self.rows, LANES)
        shift = self.ny.bit_length() - 1
        lane = iota(shape, 1)
        place = iota(shape, 0) + (lane >> shift) + (lane & (self.ny - 1)) + self.odd + step
        even = (place & 1) == 0
        other = (place & 1) == 1
        for t, here, spun, after, before in self.sides(first, last):
            fresh = (self.f[t] + self.beside(t, here, spun, after, before)) * self.inv[t]
            mask = other if (self.ny == LANES and t % 2 == 1) else even
            self.u[t + self.off] = jnp.where(mask, fresh, here)

    def smooth(self):
        if self.ny == LANES:
            for step in range(4):
                self.half_sweep(step, self.first + step, self.last - step)
        else:
            @pl.loop(0, 4)
            def _(step):
                self.half_sweep(step, self.first, self.last)

    def defects(self, first, last):
        return [
            self.f[t] - (self.diag[t] * here - self.beside(t, here, spun, after, before))
            for t, here, spun, after, before in self.sides(first, last)
        ]


def kernel(wide, narrow, rhs, cond, guess, pressure, residual, *scratch):
    (ins, corner_out, corner_in, side_in, p0, u0r, op0, a1, u1r, u1, op1, a2, own2, g2, u2, op2, a3, op3, down0, up0, down1, up1, down2, up2,
     in_sem, send0, recv0, send1, recv1, send2, recv2) = scratch
    w = lax.axis_index("wide")
    n = lax.axis_index("narrow")
    bx, bz, _ = rhs.shape
    hx, hz = bx // 2, bz // 2
    own_z = pl.ds(DEEP, bz)
    own_x = pl.ds(SIDE, bx)
    tiles_own = hz // 2
    f32 = jnp.float32

    loads = [pltpu.make_async_copy(ref, ins.at[i], in_sem.at[i]) for i, ref in enumerate((cond, rhs, guess))]
    for load in loads:
        load.start()

    for ref in (p0, u0r, a1, u1r):
        ref[...] = jnp.zeros(ref.shape, f32)
    u1[...] = jnp.zeros(u1.shape, f32)

    def valid(dw):
        return (w + dw >= 0) & (w + dw < wide)

    def when(cond_, body):
        if cond_ is True:
            body()
        else:
            pl.when(cond_)(body)

    barrier = pltpu.get_barrier_semaphore()

    def greet(dev):
        pl.semaphore_signal(barrier, inc=1, device_id=dev, device_id_type=MESH)

    for j in range(1, narrow):
        greet((w, lax.rem(n + j, narrow)))
    for dw in (-1, 1):
        @pl.when(valid(dw))
        def _(dw=dw):
            for j in range(narrow):
                greet((w + dw, lax.rem(n + j, narrow)))

    @pl.loop(0, wide)
    def _(other):
        @pl.when((other < w - 1) | (other > w + 1))
        def _():
            greet((other, n))

    for i in range(3):
        loads[i].wait()
        for z in range(bz):
            p0[i, DEEP + z, SIDE:SIDE + bx, :] = ins[i, :, z, :]

    def to_level_1(index, slices, factor):
        pairs = beside_each([slices[2 * i] + slices[2 * i + 1] for i in range(hz)])
        thin = map_rows(down_rows(bx), pairs)
        flat = stacked([thin[:, 2 * LANES * tt:2 * LANES * (tt + 1)] for tt in range(tiles_own)])
        done = factor * map_lanes(flat, down0[...])
        for tt in range(tiles_own):
            a1[index, n * tiles_own + tt, SIDE:SIDE + hx, :] = done[hx * tt:hx * (tt + 1)]

    zs = {1: (DEEP + bz - DEEP, 0, DEEP), -1: (DEEP, DEEP + bz, DEEP), 0: (DEEP, DEEP, bz)}
    xs = {1: (SIDE + bx - SIDE, 0, SIDE), -1: (SIDE, SIDE + bx, SIDE), 0: (SIDE, SIDE, bx)}
    around = [(0, 1), (0, -1), (1, 0), (-1, 0), (1, 1), (1, -1), (-1, 1), (-1, -1)]

    def has(dw, dn):
        good = None
        if dw:
            good = valid(dw)
        if dn:
            zgood = (n + dn >= 0) & (n + dn < narrow)
            good = zgood if good is None else good & zgood
        return good

    sizes = [(0, dz, DEEP - dz) for dz in range(1, DEEP)]
    sizes += [(2, dz, DEEP - dz) for dz in range(1, DEEP)]
    sizes += [(1, dz, DEEP - 1 - dz) for dz in range(1, DEEP - 1)]
    slots = []
    for which, dz, count in sizes:
        slots.append((which, dz, count, sum(slot[2] for slot in slots)))
    corners = [(-1, -1), (-1, 1), (1, -1), (1, 1)]

    for c, (dw, dn) in enumerate(corners):
        for i, dz, count, at in slots:
            z = bz - dz if dn == 1 else dz - 1
            x = bx - count if dw == 1 else 0
            corner_out[c, at:at + count, :] = ins[i, x:x + count, z, :]

    def corner_unpack(dw, dn):
        c = corners.index((-dw, -dn))
        for i, dz, count, at in slots:
            z = DEEP - dz if dn == -1 else DEEP + bz + dz - 1
            x = SIDE - count if dw == -1 else SIDE + bx
            p0[i, z, x:x + count, :] = corner_in[c, at:at + count, :]

    def side_unpack(which, dw):
        at = SIDE - DEEP if dw == -1 else SIDE + bx
        for i in ((0,), (1, 2))[which]:
            for z in range(bz):
                p0[i, DEEP + z, at:at + DEEP, :] = side_in[(dw + 1) // 2, i, :, z, :]

    def fine_refs(which, dw, dn):
        if which < 2 and dw and dn:
            c = corners.index((dw, dn))
            return corner_out.at[c], corner_in.at[c]
        arrays = (pl.ds(0, 1), pl.ds(1, 2), None)[which]
        if which < 2 and dw:
            return ins.at[arrays, pl.ds(bx - DEEP if dw == 1 else 0, DEEP)], side_in.at[(1 - dw) // 2, arrays]
        src_z, dst_z, len_z = zs[dn]
        src_x, dst_x, len_x = xs[dw]
        ref = u0r if which == 2 else p0
        lead = () if which == 2 else (arrays,)
        return (ref.at[lead + (pl.ds(src_z, len_z), pl.ds(src_x, len_x))],
                ref.at[lead + (pl.ds(dst_z, len_z), pl.ds(dst_x, len_x))])

    def fine(which, dw, dn):
        src, dst = fine_refs(which, dw, dn)
        mine = (dw + 1) * 3 + dn + 1
        theirs = (1 - dw) * 3 + 1 - dn
        return pltpu.make_async_remote_copy(
            src_ref=src, dst_ref=dst, send_sem=send0.at[which, mine], recv_sem=recv0.at[which, theirs],
            device_id=(w + dw, n + dn), device_id_type=MESH)

    def fine_in(which, dw, dn):
        _, dst = fine_refs(which, -dw, -dn)
        mine = (dw + 1) * 3 + dn + 1
        return pltpu.make_async_remote_copy(
            src_ref=dst, dst_ref=dst, send_sem=send0.at[which, mine], recv_sem=recv0.at[which, mine],
            device_id=(w + dw, n + dn), device_id_type=MESH)

    def fine_each(which, fun):
        for dw, dn in around:
            if which != 1 or not (dw and dn):
                pl.when(has(dw, dn))(lambda dw=dw, dn=dn: fun(dw, dn))

    def fine_start(which):
        fine_each(which, lambda dw, dn: fine(which, dw, dn).start())

    def fine_recv(which):
        def take(dw, dn):
            fine_in(which, dw, dn).wait_recv()
            if which < 2 and dw and dn:
                corner_unpack(dw, dn)
            elif which < 2 and dw:
                side_unpack(which, dw)
        fine_each(which, take)

    def fine_sent(which):
        fine_each(which, lambda dw, dn: fine(which, dw, dn).wait_send())

    mid = [(dw, j) for dw in (0, -1, 1) for j in range(narrow) if (dw, j) != (0, 0)]

    def mid_ref(which):
        return u1r if which == 2 else a1.at[which]

    def middle(which, dw, j):
        ref = mid_ref(which)
        tile = pl.ds(n * tiles_own, tiles_own)
        return pltpu.make_async_remote_copy(
            src_ref=ref.at[tile, pl.ds(SIDE, hx)], dst_ref=ref.at[tile, pl.ds(SIDE - dw * hx, hx)],
            send_sem=send1.at[which, dw + 1], recv_sem=recv1.at[which, 1 - dw],
            device_id=(w + dw, lax.rem(n + j, narrow)), device_id_type=MESH)

    def middle_all(which, dw):
        count = narrow if dw else narrow - 1
        every = mid_ref(which).at[pl.ds(0, count * tiles_own), pl.ds(SIDE + dw * hx, hx)]
        return pltpu.make_async_remote_copy(
            src_ref=every, dst_ref=every, send_sem=send1.at[which, dw + 1], recv_sem=recv1.at[which, dw + 1],
            device_id=(w + dw, lax.rem(n + 1, narrow)), device_id_type=MESH)

    def mid_start(which):
        for dw, j in mid:
            if dw == 0:
                middle(which, dw, j).start()
        for dw in (-1, 1):
            @pl.when(valid(dw))
            def _(dw=dw):
                for j in range(narrow):
                    middle(which, dw, j).start()

    def mid_recv(which):
        middle_all(which, 0).wait_recv()
        for dw in (-1, 1):
            pl.when(valid(dw))(lambda dw=dw: middle_all(which, dw).wait_recv())

    def mid_sent(which):
        middle_all(which, 0).wait_send()
        for dw in (-1, 1):
            pl.when(valid(dw))(lambda dw=dw: middle_all(which, dw).wait_send())

    def top(which, step):
        other = lax.rem(w + step, wide)
        return pltpu.make_async_remote_copy(
            src_ref=own2.at[which], dst_ref=g2.at[which, w], send_sem=send2.at[which],
            recv_sem=recv2.at[which], device_id=(other, n), device_id_type=MESH)

    def top_all(which):
        every = g2.at[which, pl.ds(0, wide - 1)]
        return pltpu.make_async_remote_copy(
            src_ref=every, dst_ref=every, send_sem=send2.at[which], recv_sem=recv2.at[which],
            device_id=(lax.rem(w + 1, wide), n), device_id_type=MESH)

    def top_start(which):
        @pl.loop(1, wide)
        def _(step):
            top(which, step).start()

    near = jnp.where(w > 0, 1, 0) + jnp.where(w < wide - 1, 1, 0)
    pl.semaphore_wait(barrier, (wide - 1 - near) + near * narrow + narrow - 1)

    fine_start(0)
    fine_start(1)

    names = range(6)
    ny1, ny2, ny3 = LANES // 2, LANES // 4, LANES // 8
    tiles2 = a1.shape[1] // 4
    bf16 = jnp.bfloat16
    down0[...] = stacked([down_lanes(i, LANES) for i in (0, 2)]).astype(bf16)
    up0[...] = beside_each([up_lanes(i, LANES) for i in (0, 2)]).astype(bf16)
    down1[...] = stacked([down_lanes(i, ny1) for i in range(4)]).astype(bf16)
    up1[...] = beside_each([up_lanes(i, ny1) for i in range(4)]).astype(bf16)
    down2[...] = stacked([down_lanes(i, ny2) for i in range(tiles2)]).astype(bf16)
    up2[...] = beside_each([up_lanes(i, ny2) for i in range(tiles2)]).astype(bf16)
    to_level_1(0, [p0[0, DEEP + z, SIDE:SIDE + bx, :] for z in range(bz)], 0.125)
    fine_recv(0)
    zero_level = Level(p0.at[0], p0.at[1], p0.at[2], *[op0.at[i] for i in names], LANES, 1, 2 * DEEP + bz - 1, odd=1)
    zero_level.operator()
    fine_recv(1)
    mid_start(0)
    fine_sent(0)
    fine_sent(1)
    zero_level.smooth()
    to_level_1(1, [v[SIDE:SIDE + bx] for v in zero_level.defects(DEEP, DEEP + bz)], 0.5)
    mid_start(1)
    u0r[own_z, own_x, :] = p0[2, own_z, own_x, :]

    mid_recv(0)
    one_level = Level(a1.at[0], a1.at[1], u1, *[op1.at[i] for i in names], ny1, 0, a1.shape[1], off=PAD)
    rows2 = hx // 2

    def to_level_2(which, tiles, factor):
        flat = stacked([beside_each(tiles[4 * big:4 * big + 4]) for big in range(tiles2)])
        pack = factor * map_rows(down_rows(tiles2 * hx), map_lanes(flat, down1[...]))
        own2[which] = pack
        g2[which, w] = pack

    to_level_2(0, [a1[0, t, SIDE:SIDE + hx, :] for t in range(a1.shape[1])], 0.125)
    top_start(0)
    one_level.operator()
    mid_recv(1)
    one_level.smooth()
    to_level_2(1, [v[SIDE:SIDE + hx] for v in one_level.defects(0, a1.shape[1])], 0.5)
    top_start(1)
    u1r[pl.ds(n * tiles_own, tiles_own), SIDE:SIDE + hx, :] = u1[pl.ds(PAD + n * tiles_own, tiles_own), SIDE:SIDE + hx, :]

    def unpack(which):
        for other in range(wide):
            for t in range(tiles2):
                a2[which, t, other * rows2:(other + 1) * rows2, :] = g2[which, other, t * rows2:(t + 1) * rows2, :]

    top_all(0).wait_recv()
    unpack(0)
    two_level = Level(a2.at[0], a2.at[1], u2, *[op2.at[i] for i in names], ny2, 0, tiles2)
    two_level.operator()
    all2, all3 = a2.shape[2], a3.shape[2]

    def to_level_3(tiles, factor):
        return factor * map_rows(down_rows(all2), map_lanes(beside_each(tiles), down2[...]))

    a3[0, 0] = to_level_3([a2[0, t] for t in range(tiles2)], 0.125)
    last = Level(a3.at[0], a3.at[1], a3.at[1], *[op3.at[i] for i in names], ny3, 0, 1)
    last.operator()
    mid_sent(0)
    mid_sent(1)
    top_all(0).wait_send()
    u2[...] = jnp.zeros(u2.shape, f32)
    top_all(1).wait_recv()
    mid_start(2)
    fine_start(2)
    unpack(1)
    two_level.smooth()
    source = to_level_3(two_level.defects(0, tiles2), 0.5)

    def image(v):
        spun = last.spin(v)
        return last.diag[0] * v - last.beside(0, v, spun, spun, spun)

    def total(v):
        return jnp.broadcast_to(jnp.sum(jnp.sum(v, axis=0, keepdims=True), axis=1, keepdims=True), (8, LANES))

    def tall(v):
        return jnp.concatenate([v] * (all3 // 8), axis=0)

    def advance(step, carry):
        answer, remain, wave, search, moved, twice, norm_inverse, rate = carry
        norm = total(remain * remain)
        cross = total(wave * remain)
        ahead = image(wave)
        beta = norm * norm_inverse
        below = cross - beta * (norm * rate)
        alpha = tall(norm / below)
        beta = tall(beta)
        norm_inverse = 1.0 / norm
        rate = below * norm_inverse
        twice = ahead + beta * twice
        moved = wave + beta * moved
        search = remain + beta * search
        answer = answer + alpha * search
        remain = remain - alpha * moved
        wave = wave - alpha * twice
        return answer, remain, wave, search, moved, twice, norm_inverse, rate

    nothing = jnp.zeros_like(source)
    short = jnp.zeros((8, LANES), f32)
    carry = (nothing, source, image(source), nothing, nothing, nothing, short, short)
    solved = lax.fori_loop(0, ITERS, advance, carry)[0]

    wider = map_lanes(map_rows(up_rows(all2, all3, 0), solved), up2[...])
    for t in range(tiles2):
        u2[t] = u2[t] + wider[:, LANES * t:LANES * (t + 1)]
    two_level.smooth()

    window = a1.shape[2]
    pick = up_rows(window, all2, w * rows2 - SIDE // 2)
    thin = map_rows(pick, beside_each([u2[t] for t in range(tiles2)]))
    grown = map_lanes(stacked([thin[:, LANES * t:LANES * (t + 1)] for t in range(tiles2)]), up1[...])
    top_all(1).wait_send()
    mid_sent(2)
    mid_recv(2)
    for t in range(a1.shape[1]):
        big, i = t // 4, t % 4
        u1[PAD + t] = u1r[t] + grown[window * big:window * (big + 1), LANES * i:LANES * (i + 1)]
    one_level.smooth()

    pick0 = up_rows(bx + 2 * SIDE, window, SIDE // 2)
    low, high = -DEEP // 4, (bz + DEEP - 1) // 4
    thin = map_rows(pick0, beside_each([u1[PAD + n * tiles_own + key] for key in range(low, high + 1)]))
    span = thin.shape[0]
    grown = map_lanes(stacked([thin[:, LANES * t:LANES * (t + 1)] for t in range(high + 1 - low)]), up0[...])
    fine_sent(2)
    fine_recv(2)
    for zi in range(2 * DEEP + bz):
        t = (zi - DEEP) // 4 - low
        side = ((zi - DEEP) % 4) // 2
        p0[2, zi] = u0r[zi] + grown[span * t:span * (t + 1), LANES * side:LANES * (side + 1)]
    zero_level.smooth()
    for z, left in enumerate(zero_level.defects(DEEP, DEEP + bz)):
        pressure[:, z, :] = p0[2, DEEP + z, SIDE:SIDE + bx, :]
        residual[:, z, :] = left[SIDE:SIDE + bx]


def local(wide, narrow, rhs, coefficient, guess):
    bx, bz, by = rhs.shape
    hx = bx // 2
    z0 = bz + 2 * DEEP
    x0 = bx + 2 * SIDE
    t1 = narrow * bz // 4
    x1 = hx + 2 * SIDE
    t2 = t1 // 4
    x2 = wide * bx // 4
    x3 = x2 // 2
    vmem = lambda *shape: pltpu.VMEM(shape, jnp.float32)
    half = lambda *shape: pltpu.VMEM(shape, jnp.bfloat16)
    dma = lambda *shape: pltpu.SemaphoreType.DMA(shape)
    out = jax.ShapeDtypeStruct(rhs.shape, jnp.float32)
    return pl.pallas_call(
        functools.partial(kernel, wide, narrow),
        out_shape=(out, out),
        in_specs=[pl.BlockSpec(memory_space=pltpu.HBM)] * 3,
        out_specs=[pl.BlockSpec(memory_space=pltpu.VMEM)] * 2,
        scratch_shapes=[
            vmem(3, bx, bz, by), vmem(4, 32, LANES), vmem(4, 32, LANES), vmem(2, 3, DEEP, bz, by),
            vmem(3, z0, x0, by), vmem(z0, x0, by), vmem(6, z0, x0, by),
            vmem(2, t1, x1, LANES), vmem(t1, x1, LANES), vmem(t1 + 2 * PAD, x1, LANES), vmem(6, t1, x1, LANES),
            vmem(2, t2, x2, LANES), vmem(2, t2 * hx // 2, LANES), vmem(2, wide, t2 * hx // 2, LANES),
            vmem(t2, x2, LANES), vmem(6, t2, x2, LANES),
            vmem(2, 1, x3, LANES), vmem(6, 1, x3, LANES),
            half(2 * LANES, LANES), half(LANES, 2 * LANES), half(4 * LANES, LANES), half(LANES, 4 * LANES),
            half(t2 * LANES, LANES), half(LANES, t2 * LANES),
            dma(3), dma(3, 9), dma(3, 9), dma(3, 3), dma(3, 3), dma(2), dma(2),
        ],
        compiler_params=pltpu.CompilerParams(collective_id=0, has_side_effects=True, vmem_limit_bytes=48 * 2**20),
    )(rhs, coefficient, guess)


def solution(mesh):
    spec = P("wide", "narrow", None)
    return jax.shard_map(
        functools.partial(local, mesh.shape["wide"], mesh.shape["narrow"]),
        mesh=mesh,
        in_specs=(spec, spec, spec),
        out_specs=(spec, spec),
        check_vma=False,
    )
```

```python
import functools

import jax
import jax.numpy as jnp
from jax import lax
from jax.experimental import pallas as pl
from jax.experimental.pallas import tpu as pltpu
from jax.sharding import PartitionSpec as P

ITERS = 20
LANES = 128
DEEP = 5
SIDE = 8
PAD = 2
MESH = pl.DeviceIdType.MESH


def dot(a, b):
    return lax.dot_general(a, b, (((1,), (0,)), ((), ())), preferred_element_type=jnp.float32)


def split(a):
    high = a.astype(jnp.bfloat16).astype(jnp.float32)
    rest = a - high
    mid = rest.astype(jnp.bfloat16).astype(jnp.float32)
    return jnp.concatenate([high, mid, rest - mid], axis=0).astype(jnp.bfloat16)


def map_lanes(a, matrix):
    rows = a.shape[0]
    out = dot(split(a), matrix)
    return out[:rows] + (out[rows:2 * rows] + out[2 * rows:])


def map_rows(matrix, a):
    return dot(jnp.concatenate([matrix, matrix, matrix], axis=1).astype(jnp.bfloat16), split(a))


def beside_each(parts):
    return jnp.concatenate(parts, axis=1)


def stacked(parts):
    return jnp.concatenate(parts, axis=0)


def iota(shape, dim):
    return lax.broadcasted_iota(jnp.int32, shape, dim)


def one(cond):
    return jnp.where(cond, 1.0, 0.0).astype(jnp.float32)


def coarse_lane(lane, part, ny):
    shift = ny.bit_length() - 1
    z = part * (LANES // ny) + (lane >> shift)
    return (z >> 1) * (ny // 2) + ((lane & (ny - 1)) >> 1)


def down_lanes(part, ny):
    shape = (LANES, LANES)
    return one(iota(shape, 1) == coarse_lane(iota(shape, 0), part, ny))


def up_lanes(part, ny):
    shape = (LANES, LANES)
    return one(iota(shape, 0) == coarse_lane(iota(shape, 1), part, ny))


def down_rows(rows):
    shape = (rows // 2, rows)
    return one(iota(shape, 0) == (iota(shape, 1) >> 1))


def up_rows(rows, coarse, first):
    shape = (rows, coarse)
    return one(iota(shape, 1) == (iota(shape, 0) >> 1) + first)


class Level:
    def __init__(self, k, f, u, wx, wy, wzp, wzm, diag, inv, ny, first, last, off=0, odd=0):
        self.k, self.f, self.u = k, f, u
        self.wx, self.wy, self.wzp, self.wzm, self.diag, self.inv = wx, wy, wzp, wzm, diag, inv
        self.ny, self.first, self.last, self.off, self.odd = ny, first, last, off, odd
        self.rows = k.shape[1]
        self.tiles = k.shape[0]

    def spin(self, v):
        if self.ny == LANES:
            return v, v
        down = pltpu.roll(v, LANES - self.ny, 1)
        return down, (down if 2 * self.ny == LANES else pltpu.roll(v, self.ny, 1))

    def above(self, here, after):
        if self.ny == LANES:
            return after[0]
        return jnp.where(iota(here[0].shape, 1) < LANES - self.ny, here[0], after[0])

    def below(self, here, before):
        if self.ny == LANES:
            return before[1]
        return jnp.where(iota(here[0].shape, 1) >= self.ny, here[1], before[1])

    def operator(self):
        shape = (self.rows, LANES)
        row = iota(shape, 0)
        y = iota(shape, 1) & (self.ny - 1)
        zero = jnp.zeros(shape, jnp.float32)
        for t in range(self.first, self.last):
            k = self.k[t]
            spun = self.spin(k)
            after = self.spin(self.k[t + 1] if t + 1 < self.tiles else zero)
            before = self.spin(self.k[t - 1] if t > 0 else zero)
            xp = jnp.where(row == self.rows - 1, 0.0, pltpu.roll(k, self.rows - 1, 0))
            xm = jnp.where(row == 0, 0.0, pltpu.roll(k, 1, 0))
            yp = jnp.where(y == self.ny - 1, 0.0, pltpu.roll(k, LANES - 1, 1))
            ym = jnp.where(y == 0, 0.0, pltpu.roll(k, 1, 1))
            zp = self.above(spun, after)
            zm = self.below(spun, before)
            diag = 3.0 * k + 0.5 * (xp + xm + zp + zm + yp + ym)
            diag = jnp.where(diag > 0.0, diag, 1.0)
            live = k > 0.0

            def face(other):
                return jnp.where(live & (other > 0.0), 0.5 * (k + other), 0.0)

            self.wx[t] = face(xp)
            self.wy[t] = face(yp)
            self.wzp[t] = face(zp)
            self.wzm[t] = face(zm)
            self.diag[t] = diag
            self.inv[t] = 1.0 / diag

    def beside(self, t, here, spun, after, before):
        wx = self.wx[t]
        wy = self.wy[t]
        total = self.wzp[t] * self.above(spun, after) + self.wzm[t] * self.below(spun, before)
        total = total + (wx * pltpu.roll(here, self.rows - 1, 0) + pltpu.roll(wx * here, 1, 0))
        return total + (wy * pltpu.roll(here, LANES - 1, 1) + pltpu.roll(wy * here, 1, 1))

    def sides(self, first, last):
        here = self.u[first + self.off]
        spun = self.spin(here)
        before = self.spin(self.u[first - 1 + self.off]) if first > 0 else spun
        for t in range(first, last):
            if t + 1 < self.tiles:
                later = self.u[t + 1 + self.off]
                after = self.spin(later)
            else:
                later, after = here, spun
            yield t, here, spun, after, before
            here, before, spun = later, spun, after

    def half_sweep(self, step, first, last, blank=False):
        shape = (self.rows, LANES)
        shift = self.ny.bit_length() - 1
        lane = iota(shape, 1)
        place = iota(shape, 0) + (lane >> shift) + (lane & (self.ny - 1)) + self.odd + step
        even = (place & 1) == 0
        other = (place & 1) == 1
        if blank:
            for t in range(first, last):
                self.u[t + self.off] = jnp.where(even, self.f[t] * self.inv[t], 0.0)
            return
        for t, here, spun, after, before in self.sides(first, last):
            fresh = (self.f[t] + self.beside(t, here, spun, after, before)) * self.inv[t]
            mask = other if (self.ny == LANES and t % 2 == 1) else even
            self.u[t + self.off] = jnp.where(mask, fresh, here)

    def smooth(self, blank=False):
        if self.ny == LANES:
            for step in range(4):
                self.half_sweep(step, self.first + step, self.last - step)
            return
        if blank:
            self.half_sweep(0, self.first, self.last, blank=True)
        if self.rows <= 64:
            for step in range(1 if blank else 0, 4):
                self.half_sweep(step, self.first, self.last)
        else:
            @pl.loop(1 if blank else 0, 4)
            def _(step):
                self.half_sweep(step, self.first, self.last)

    def defects(self, first, last):
        return [
            self.f[t] - (self.diag[t] * here - self.beside(t, here, spun, after, before))
            for t, here, spun, after, before in self.sides(first, last)
        ]


def kernel(wide, narrow, rhs, cond, guess, pressure, residual, *scratch):
    (ins, corner_out, corner_in, side_in, p0, u0r, op0, a1, u1r, u1, op1, a2, own2, g2, u2, op2, a3, op3, down0, up0, down1, up1, down2, up2,
     in_sem, send0, recv0, send1, recv1, send2, recv2) = scratch
    w = lax.axis_index("wide")
    n = lax.axis_index("narrow")
    bx, bz, _ = rhs.shape
    hx, hz = bx // 2, bz // 2
    own_z = pl.ds(DEEP, bz)
    own_x = pl.ds(SIDE, bx)
    tiles_own = hz // 2
    f32 = jnp.float32

    loads = [pltpu.make_async_copy(ref, ins.at[i], in_sem.at[i]) for i, ref in enumerate((cond, rhs, guess))]
    for load in loads:
        load.start()

    def valid(dw):
        return (w + dw >= 0) & (w + dw < wide)

    def when(cond_, body):
        if cond_ is True:
            body()
        else:
            pl.when(cond_)(body)

    barrier = pltpu.get_barrier_semaphore()

    def greet(dev):
        pl.semaphore_signal(barrier, inc=1, device_id=dev, device_id_type=MESH)

    for j in range(1, narrow):
        greet((w, lax.rem(n + j, narrow)))
    for dw in (-1, 1):
        @pl.when(valid(dw))
        def _(dw=dw):
            for j in range(narrow):
                greet((w + dw, lax.rem(n + j, narrow)))

    @pl.loop(0, wide)
    def _(other):
        @pl.when((other < w - 1) | (other > w + 1))
        def _():
            greet((other, n))

    def clear(ref):
        ref[...] = jnp.zeros(ref.shape, f32)

    lower, upper = pl.ds(0, SIDE), pl.ds(SIDE + bx, SIDE)
    clear(p0.at[:, :, lower])
    clear(p0.at[:, :, upper])
    pl.when(n == 0)(lambda: clear(p0.at[:, pl.ds(0, DEEP), own_x]))
    pl.when(n == narrow - 1)(lambda: clear(p0.at[:, pl.ds(DEEP + bz, DEEP), own_x]))
    for at, dw in ((0, -1), (SIDE + hx, 1)):
        @pl.when(jnp.logical_not(valid(dw)))
        def _(at=at):
            clear(a1.at[:, :, pl.ds(at, SIDE)])
            clear(u1r.at[:, pl.ds(at, SIDE)])
    clear(u1.at[pl.ds(0, PAD)])
    clear(u1.at[pl.ds(PAD + u1r.shape[0], PAD)])

    for i in range(3):
        loads[i].wait()
        for z in range(bz):
            p0[i, DEEP + z, SIDE:SIDE + bx, :] = ins[i, :, z, :]

    def to_level_1(index, slices, factor):
        pairs = beside_each([slices[2 * i] + slices[2 * i + 1] for i in range(hz)])
        thin = map_rows(down_rows(bx), pairs)
        flat = stacked([thin[:, 2 * LANES * tt:2 * LANES * (tt + 1)] for tt in range(tiles_own)])
        done = factor * map_lanes(flat, down0[...])
        for tt in range(tiles_own):
            a1[index, n * tiles_own + tt, SIDE:SIDE + hx, :] = done[hx * tt:hx * (tt + 1)]

    zs = {1: (DEEP + bz - DEEP, 0, DEEP), -1: (DEEP, DEEP + bz, DEEP), 0: (DEEP, DEEP, bz)}
    xs = {1: (SIDE + bx - SIDE, 0, SIDE), -1: (SIDE, SIDE + bx, SIDE), 0: (SIDE, SIDE, bx)}
    around = [(1, 0), (-1, 0), (1, 1), (1, -1), (-1, 1), (-1, -1), (0, 1), (0, -1)]

    def has(dw, dn):
        good = None
        if dw:
            good = valid(dw)
        if dn:
            zgood = (n + dn >= 0) & (n + dn < narrow)
            good = zgood if good is None else good & zgood
        return good

    sizes = [(0, dz, DEEP - dz) for dz in range(1, DEEP)]
    sizes += [(2, dz, DEEP - dz) for dz in range(1, DEEP)]
    sizes += [(1, dz, DEEP - 1 - dz) for dz in range(1, DEEP - 1)]
    slots = []
    for which, dz, count in sizes:
        slots.append((which, dz, count, sum(slot[2] for slot in slots)))
    corners = [(-1, -1), (-1, 1), (1, -1), (1, 1)]

    for c, (dw, dn) in enumerate(corners):
        for i, dz, count, at in slots:
            z = bz - dz if dn == 1 else dz - 1
            x = bx - count if dw == 1 else 0
            corner_out[c, at:at + count, :] = ins[i, x:x + count, z, :]

    def corner_unpack(dw, dn):
        c = corners.index((-dw, -dn))
        for i, dz, count, at in slots:
            z = DEEP - dz if dn == -1 else DEEP + bz + dz - 1
            x = SIDE - count if dw == -1 else SIDE + bx
            p0[i, z, x:x + count, :] = corner_in[c, at:at + count, :]

    def side_unpack(which, dw):
        at = SIDE - DEEP if dw == -1 else SIDE + bx
        for i in ((0,), (1, 2))[which]:
            for z in range(bz):
                p0[i, DEEP + z, at:at + DEEP, :] = side_in[(dw + 1) // 2, i, :, z, :]

    def fine_refs(which, dw, dn):
        if which < 2 and dw and dn:
            c = corners.index((dw, dn))
            return corner_out.at[c], corner_in.at[c]
        arrays = (pl.ds(0, 1), pl.ds(1, 2), None)[which]
        if which < 2 and dw:
            return ins.at[arrays, pl.ds(bx - DEEP if dw == 1 else 0, DEEP)], side_in.at[(1 - dw) // 2, arrays]
        src_z, dst_z, len_z = zs[dn]
        src_x, dst_x, len_x = xs[dw]
        ref = u0r if which == 2 else p0
        lead = () if which == 2 else (arrays,)
        return (ref.at[lead + (pl.ds(src_z, len_z), pl.ds(src_x, len_x))],
                ref.at[lead + (pl.ds(dst_z, len_z), pl.ds(dst_x, len_x))])

    def fine(which, dw, dn):
        src, dst = fine_refs(which, dw, dn)
        mine = (dw + 1) * 3 + dn + 1
        theirs = (1 - dw) * 3 + 1 - dn
        return pltpu.make_async_remote_copy(
            src_ref=src, dst_ref=dst, send_sem=send0.at[which, mine], recv_sem=recv0.at[which, theirs],
            device_id=(w + dw, n + dn), device_id_type=MESH)

    def fine_in(which, dw, dn):
        _, dst = fine_refs(which, -dw, -dn)
        mine = (dw + 1) * 3 + dn + 1
        return pltpu.make_async_remote_copy(
            src_ref=dst, dst_ref=dst, send_sem=send0.at[which, mine], recv_sem=recv0.at[which, mine],
            device_id=(w + dw, n + dn), device_id_type=MESH)

    def fine_each(which, fun):
        for dw, dn in around:
            if which != 1 or not (dw and dn):
                pl.when(has(dw, dn))(lambda dw=dw, dn=dn: fun(dw, dn))

    def fine_start(which):
        fine_each(which, lambda dw, dn: fine(which, dw, dn).start())

    def fine_recv(which):
        def take(dw, dn):
            fine_in(which, dw, dn).wait_recv()
            if which < 2 and dw and dn:
                corner_unpack(dw, dn)
            elif which < 2 and dw:
                side_unpack(which, dw)
        fine_each(which, take)

    def fine_sent(which):
        fine_each(which, lambda dw, dn: fine(which, dw, dn).wait_send())

    def mid_ref(which):
        return u1r if which == 2 else a1.at[which]

    def middle(which, dw, j):
        ref = mid_ref(which)
        tile = pl.ds(n * tiles_own, tiles_own)
        return pltpu.make_async_remote_copy(
            src_ref=ref.at[tile, pl.ds(SIDE, hx)], dst_ref=ref.at[tile, pl.ds(SIDE - dw * hx, hx)],
            send_sem=send1.at[which, dw + 1], recv_sem=recv1.at[which, 1 - dw],
            device_id=(w + dw, lax.rem(n + j, narrow)), device_id_type=MESH)

    def middle_all(which, dw):
        count = narrow if dw else narrow - 1
        every = mid_ref(which).at[pl.ds(0, count * tiles_own), pl.ds(SIDE + dw * hx, hx)]
        return pltpu.make_async_remote_copy(
            src_ref=every, dst_ref=every, send_sem=send1.at[which, dw + 1], recv_sem=recv1.at[which, dw + 1],
            device_id=(w + dw, lax.rem(n + 1, narrow)), device_id_type=MESH)

    def mid_start(which):
        for dw in (-1, 1):
            @pl.when(valid(dw))
            def _(dw=dw):
                for j in range(narrow):
                    middle(which, dw, j).start()
        for j in range(1, narrow):
            middle(which, 0, j).start()

    def mid_recv(which):
        middle_all(which, 0).wait_recv()
        for dw in (-1, 1):
            pl.when(valid(dw))(lambda dw=dw: middle_all(which, dw).wait_recv())

    def mid_sent(which):
        middle_all(which, 0).wait_send()
        for dw in (-1, 1):
            pl.when(valid(dw))(lambda dw=dw: middle_all(which, dw).wait_send())

    def top(which, step):
        other = lax.rem(w + step, wide)
        return pltpu.make_async_remote_copy(
            src_ref=own2.at[which], dst_ref=g2.at[which, w], send_sem=send2.at[which],
            recv_sem=recv2.at[which], device_id=(other, n), device_id_type=MESH)

    def top_all(which):
        every = g2.at[which, pl.ds(0, wide - 1)]
        return pltpu.make_async_remote_copy(
            src_ref=every, dst_ref=every, send_sem=send2.at[which], recv_sem=recv2.at[which],
            device_id=(lax.rem(w + 1, wide), n), device_id_type=MESH)

    def top_start(which):
        @pl.loop(1, wide)
        def _(step):
            top(which, step).start()

    near = jnp.where(w > 0, 1, 0) + jnp.where(w < wide - 1, 1, 0)
    pl.semaphore_wait(barrier, (wide - 1 - near) + near * narrow + narrow - 1)

    fine_start(0)
    fine_start(1)
    for dw, dn in around:
        pl.when(jnp.logical_not(has(dw, dn)))(lambda dw=dw, dn=dn: clear(fine_refs(2, -dw, -dn)[1]))

    names = range(6)
    ny1, ny2, ny3 = LANES // 2, LANES // 4, LANES // 8
    tiles2 = a1.shape[1] // 4
    bf16 = jnp.bfloat16
    down0[...] = stacked([down_lanes(i, LANES) for i in (0, 2)]).astype(bf16)
    up0[...] = beside_each([up_lanes(i, LANES) for i in (0, 2)]).astype(bf16)
    down1[...] = stacked([down_lanes(i, ny1) for i in range(4)]).astype(bf16)
    up1[...] = beside_each([up_lanes(i, ny1) for i in range(4)]).astype(bf16)
    down2[...] = stacked([down_lanes(i, ny2) for i in range(tiles2)]).astype(bf16)
    up2[...] = beside_each([up_lanes(i, ny2) for i in range(tiles2)]).astype(bf16)
    to_level_1(0, [p0[0, DEEP + z, SIDE:SIDE + bx, :] for z in range(bz)], 0.125)
    fine_recv(0)
    zero_level = Level(p0.at[0], p0.at[1], p0.at[2], *[op0.at[i] for i in names], LANES, 1, 2 * DEEP + bz - 1, odd=1)
    zero_level.operator()
    fine_recv(1)
    mid_start(0)
    fine_sent(0)
    fine_sent(1)
    zero_level.smooth()
    to_level_1(1, [v[SIDE:SIDE + bx] for v in zero_level.defects(DEEP, DEEP + bz)], 0.5)
    mid_start(1)
    u0r[own_z, own_x, :] = p0[2, own_z, own_x, :]

    mid_recv(0)
    one_level = Level(a1.at[0], a1.at[1], u1, *[op1.at[i] for i in names], ny1, 0, a1.shape[1], off=PAD)
    rows2 = hx // 2

    def to_level_2(which, tiles, factor):
        flat = stacked([beside_each(tiles[4 * big:4 * big + 4]) for big in range(tiles2)])
        pack = factor * map_rows(down_rows(tiles2 * hx), map_lanes(flat, down1[...]))
        own2[which] = pack
        g2[which, w] = pack

    to_level_2(0, [a1[0, t, SIDE:SIDE + hx, :] for t in range(a1.shape[1])], 0.125)
    top_start(0)
    one_level.operator()
    mid_recv(1)
    one_level.smooth(blank=True)
    to_level_2(1, [v[SIDE:SIDE + hx] for v in one_level.defects(0, a1.shape[1])], 0.5)
    top_start(1)
    u1r[pl.ds(n * tiles_own, tiles_own), SIDE:SIDE + hx, :] = u1[pl.ds(PAD + n * tiles_own, tiles_own), SIDE:SIDE + hx, :]

    def unpack(which):
        for other in range(wide):
            for t in range(tiles2):
                a2[which, t, other * rows2:(other + 1) * rows2, :] = g2[which, other, t * rows2:(t + 1) * rows2, :]

    top_all(0).wait_recv()
    unpack(0)
    two_level = Level(a2.at[0], a2.at[1], u2, *[op2.at[i] for i in names], ny2, 0, tiles2)
    two_level.operator()
    all2, all3 = a2.shape[2], a3.shape[2]

    def to_level_3(tiles, factor):
        return factor * map_rows(down_rows(all2), map_lanes(beside_each(tiles), down2[...]))

    a3[0, 0] = to_level_3([a2[0, t] for t in range(tiles2)], 0.125)
    last = Level(a3.at[0], a3.at[1], a3.at[1], *[op3.at[i] for i in names], ny3, 0, 1)
    last.operator()
    mid_sent(0)
    mid_sent(1)
    top_all(0).wait_send()
    top_all(1).wait_recv()
    mid_start(2)
    fine_start(2)
    unpack(1)
    two_level.smooth(blank=True)
    source = to_level_3(two_level.defects(0, tiles2), 0.5)

    def image(v):
        spun = last.spin(v)
        return last.diag[0] * v - last.beside(0, v, spun, spun, spun)

    def total(v):
        return jnp.broadcast_to(jnp.sum(jnp.sum(v, axis=0, keepdims=True), axis=1, keepdims=True), (8, LANES))

    def tall(v):
        return jnp.concatenate([v] * (all3 // 8), axis=0)

    def advance(step, carry):
        answer, remain, wave, search, moved, twice, norm_inverse, rate = carry
        norm = total(remain * remain)
        cross = total(wave * remain)
        ahead = image(wave)
        beta = norm * norm_inverse
        below = cross - beta * (norm * rate)
        alpha = tall(norm / below)
        beta = tall(beta)
        norm_inverse = 1.0 / norm
        rate = below * norm_inverse
        twice = ahead + beta * twice
        moved = wave + beta * moved
        search = remain + beta * search
        answer = answer + alpha * search
        remain = remain - alpha * moved
        wave = wave - alpha * twice
        return answer, remain, wave, search, moved, twice, norm_inverse, rate

    nothing = jnp.zeros_like(source)
    short = jnp.zeros((8, LANES), f32)
    carry = (nothing, source, image(source), nothing, nothing, nothing, short, short)
    solved = lax.fori_loop(0, ITERS, advance, carry)[0]

    wider = map_lanes(map_rows(up_rows(all2, all3, 0), solved), up2[...])
    for t in range(tiles2):
        u2[t] = u2[t] + wider[:, LANES * t:LANES * (t + 1)]
    two_level.smooth()

    window = a1.shape[2]
    pick = up_rows(window, all2, w * rows2 - SIDE // 2)
    thin = map_rows(pick, beside_each([u2[t] for t in range(tiles2)]))
    grown = map_lanes(stacked([thin[:, LANES * t:LANES * (t + 1)] for t in range(tiles2)]), up1[...])
    top_all(1).wait_send()
    mid_sent(2)
    mid_recv(2)
    for t in range(a1.shape[1]):
        big, i = t // 4, t % 4
        u1[PAD + t] = u1r[t] + grown[window * big:window * (big + 1), LANES * i:LANES * (i + 1)]
    one_level.smooth()

    pick0 = up_rows(bx + 2 * SIDE, window, SIDE // 2)
    low, high = -DEEP // 4, (bz + DEEP - 1) // 4
    thin = map_rows(pick0, beside_each([u1[PAD + n * tiles_own + key] for key in range(low, high + 1)]))
    span = thin.shape[0]
    grown = map_lanes(stacked([thin[:, LANES * t:LANES * (t + 1)] for t in range(high + 1 - low)]), up0[...])
    fine_sent(2)
    fine_recv(2)
    for zi in range(2 * DEEP + bz):
        t = (zi - DEEP) // 4 - low
        side = ((zi - DEEP) % 4) // 2
        p0[2, zi] = u0r[zi] + grown[span * t:span * (t + 1), LANES * side:LANES * (side + 1)]
    zero_level.smooth()
    stores = [pltpu.make_async_copy(ins.at[i], ref, in_sem.at[i]) for i, ref in enumerate((pressure, residual))]
    for z in range(bz):
        ins[0, :, z, :] = p0[2, DEEP + z, SIDE:SIDE + bx, :]
    stores[0].start()
    for z, left in enumerate(zero_level.defects(DEEP, DEEP + bz)):
        ins[1, :, z, :] = left[SIDE:SIDE + bx]
    stores[1].start()
    for store in stores:
        store.wait()


def local(wide, narrow, rhs, coefficient, guess):
    bx, bz, by = rhs.shape
    hx = bx // 2
    z0 = bz + 2 * DEEP
    x0 = bx + 2 * SIDE
    t1 = narrow * bz // 4
    x1 = hx + 2 * SIDE
    t2 = t1 // 4
    x2 = wide * bx // 4
    x3 = x2 // 2
    vmem = lambda *shape: pltpu.VMEM(shape, jnp.float32)
    half = lambda *shape: pltpu.VMEM(shape, jnp.bfloat16)
    dma = lambda *shape: pltpu.SemaphoreType.DMA(shape)
    out = jax.ShapeDtypeStruct(rhs.shape, jnp.float32)
    return pl.pallas_call(
        functools.partial(kernel, wide, narrow),
        out_shape=(out, out),
        in_specs=[pl.BlockSpec(memory_space=pltpu.HBM)] * 3,
        out_specs=[pl.BlockSpec(memory_space=pltpu.HBM)] * 2,
        scratch_shapes=[
            vmem(3, bx, bz, by), vmem(4, 32, LANES), vmem(4, 32, LANES), vmem(2, 3, DEEP, bz, by),
            vmem(3, z0, x0, by), vmem(z0, x0, by), vmem(6, z0, x0, by),
            vmem(2, t1, x1, LANES), vmem(t1, x1, LANES), vmem(t1 + 2 * PAD, x1, LANES), vmem(6, t1, x1, LANES),
            vmem(2, t2, x2, LANES), vmem(2, t2 * hx // 2, LANES), vmem(2, wide, t2 * hx // 2, LANES),
            vmem(t2, x2, LANES), vmem(6, t2, x2, LANES),
            vmem(2, 1, x3, LANES), vmem(6, 1, x3, LANES),
            half(2 * LANES, LANES), half(LANES, 2 * LANES), half(4 * LANES, LANES), half(LANES, 4 * LANES),
            half(t2 * LANES, LANES), half(LANES, t2 * LANES),
            dma(3), dma(3, 9), dma(3, 9), dma(3, 3), dma(3, 3), dma(2), dma(2),
        ],
        compiler_params=pltpu.CompilerParams(collective_id=0, has_side_effects=True, vmem_limit_bytes=64 * 2**20 - 2**18),
    )(rhs, coefficient, guess)


def solution(mesh):
    spec = P("wide", "narrow", None)
    return jax.shard_map(
        functools.partial(local, mesh.shape["wide"], mesh.shape["narrow"]),
        mesh=mesh,
        in_specs=(spec, spec, spec),
        out_specs=(spec, spec),
        check_vma=False,
    )
```

```python
import functools

import jax
import jax.numpy as jnp
from jax import lax
from jax.experimental import pallas as pl
from jax.experimental.pallas import tpu as pltpu
from jax.sharding import PartitionSpec as P

ITERS = 20
LANES = 128
DEEP = 5
SIDE = 8
PAD = 2
MESH = pl.DeviceIdType.MESH


def dot(a, b):
    return lax.dot_general(a, b, (((1,), (0,)), ((), ())), preferred_element_type=jnp.float32)


def split(a):
    high = a.astype(jnp.bfloat16).astype(jnp.float32)
    rest = a - high
    mid = rest.astype(jnp.bfloat16).astype(jnp.float32)
    return jnp.concatenate([high, mid, rest - mid], axis=0).astype(jnp.bfloat16)


def map_lanes(a, matrix):
    rows = a.shape[0]
    out = dot(split(a), matrix)
    return out[:rows] + (out[rows:2 * rows] + out[2 * rows:])


def map_rows(matrix, a):
    return dot(jnp.concatenate([matrix, matrix, matrix], axis=1).astype(jnp.bfloat16), split(a))


def beside_each(parts):
    return jnp.concatenate(parts, axis=1)


def stacked(parts):
    return jnp.concatenate(parts, axis=0)


def iota(shape, dim):
    return lax.broadcasted_iota(jnp.int32, shape, dim)


def one(cond):
    return jnp.where(cond, 1.0, 0.0).astype(jnp.float32)


def coarse_lane(lane, part, ny):
    shift = ny.bit_length() - 1
    z = part * (LANES // ny) + (lane >> shift)
    return (z >> 1) * (ny // 2) + ((lane & (ny - 1)) >> 1)


def down_lanes(part, ny):
    shape = (LANES, LANES)
    return one(iota(shape, 1) == coarse_lane(iota(shape, 0), part, ny))


def up_lanes(part, ny):
    shape = (LANES, LANES)
    return one(iota(shape, 0) == coarse_lane(iota(shape, 1), part, ny))


def down_rows(rows):
    shape = (rows // 2, rows)
    return one(iota(shape, 0) == (iota(shape, 1) >> 1))


def up_rows(rows, coarse, first):
    shape = (rows, coarse)
    return one(iota(shape, 1) == (iota(shape, 0) >> 1) + first)


class Level:
    def __init__(self, k, f, u, wx, wy, wzp, wzm, diag, inv, ny, first, last, off=0, odd=0):
        self.k, self.f, self.u = k, f, u
        self.wx, self.wy, self.wzp, self.wzm, self.diag, self.inv = wx, wy, wzp, wzm, diag, inv
        self.ny, self.first, self.last, self.off, self.odd = ny, first, last, off, odd
        self.rows = k.shape[1]
        self.tiles = k.shape[0]

    def spin(self, v):
        if self.ny == LANES:
            return v, v
        down = pltpu.roll(v, LANES - self.ny, 1)
        return down, (down if 2 * self.ny == LANES else pltpu.roll(v, self.ny, 1))

    def above(self, here, after):
        if self.ny == LANES:
            return after[0]
        return jnp.where(iota(here[0].shape, 1) < LANES - self.ny, here[0], after[0])

    def below(self, here, before):
        if self.ny == LANES:
            return before[1]
        return jnp.where(iota(here[0].shape, 1) >= self.ny, here[1], before[1])

    def operator(self):
        shape = (self.rows, LANES)
        row = iota(shape, 0)
        y = iota(shape, 1) & (self.ny - 1)
        zero = jnp.zeros(shape, jnp.float32)
        for t in range(self.first, self.last):
            k = self.k[t]
            spun = self.spin(k)
            after = self.spin(self.k[t + 1] if t + 1 < self.tiles else zero)
            before = self.spin(self.k[t - 1] if t > 0 else zero)
            xp = jnp.where(row == self.rows - 1, 0.0, pltpu.roll(k, self.rows - 1, 0))
            xm = jnp.where(row == 0, 0.0, pltpu.roll(k, 1, 0))
            yp = jnp.where(y == self.ny - 1, 0.0, pltpu.roll(k, LANES - 1, 1))
            ym = jnp.where(y == 0, 0.0, pltpu.roll(k, 1, 1))
            zp = self.above(spun, after)
            zm = self.below(spun, before)
            diag = 3.0 * k + 0.5 * (xp + xm + zp + zm + yp + ym)
            diag = jnp.where(diag > 0.0, diag, 1.0)
            live = k > 0.0

            def face(other):
                return jnp.where(live & (other > 0.0), 0.5 * (k + other), 0.0)

            self.wx[t] = face(xp)
            self.wy[t] = face(yp)
            self.wzp[t] = face(zp)
            self.wzm[t] = face(zm)
            self.diag[t] = diag
            self.inv[t] = 1.0 / diag

    def beside(self, t, here, spun, after, before):
        wx = self.wx[t]
        wy = self.wy[t]
        total = self.wzp[t] * self.above(spun, after) + self.wzm[t] * self.below(spun, before)
        total = total + (wx * pltpu.roll(here, self.rows - 1, 0) + pltpu.roll(wx * here, 1, 0))
        return total + (wy * pltpu.roll(here, LANES - 1, 1) + pltpu.roll(wy * here, 1, 1))

    def sides(self, first, last):
        here = self.u[first + self.off]
        spun = self.spin(here)
        before = self.spin(self.u[first - 1 + self.off]) if first > 0 else spun
        for t in range(first, last):
            if t + 1 < self.tiles:
                later = self.u[t + 1 + self.off]
                after = self.spin(later)
            else:
                later, after = here, spun
            yield t, here, spun, after, before
            here, before, spun = later, spun, after

    def half_sweep(self, step, first, last, blank=False):
        shape = (self.rows, LANES)
        shift = self.ny.bit_length() - 1
        lane = iota(shape, 1)
        place = iota(shape, 0) + (lane >> shift) + (lane & (self.ny - 1)) + self.odd + step
        even = (place & 1) == 0
        other = (place & 1) == 1
        if blank:
            for t in range(first, last):
                self.u[t + self.off] = jnp.where(even, self.f[t] * self.inv[t], 0.0)
            return
        for t, here, spun, after, before in self.sides(first, last):
            fresh = (self.f[t] + self.beside(t, here, spun, after, before)) * self.inv[t]
            mask = other if (self.ny == LANES and t % 2 == 1) else even
            self.u[t + self.off] = jnp.where(mask, fresh, here)

    def smooth(self, blank=False):
        if self.ny == LANES:
            for step in range(4):
                self.half_sweep(step, self.first + step, self.last - step)
            return
        if blank:
            self.half_sweep(0, self.first, self.last, blank=True)
        if self.rows <= 64:
            for step in range(1 if blank else 0, 4):
                self.half_sweep(step, self.first, self.last)
        else:
            @pl.loop(1 if blank else 0, 4)
            def _(step):
                self.half_sweep(step, self.first, self.last)

    def defects(self, first, last):
        return [
            self.f[t] - (self.diag[t] * here - self.beside(t, here, spun, after, before))
            for t, here, spun, after, before in self.sides(first, last)
        ]


def kernel(wide, narrow, rhs, cond, guess, pressure, residual, *scratch):
    (ins, corner_out, corner_in, k_in, side_out, side_in, p0, u0r, op0, a1, u1r, u1, op1, a2, own2, g2, u2, op2, a3, op3, down0, up0, down1, up1, down2, up2,
     in_sem, send0, recv0, send1, recv1, send2, recv2) = scratch
    w = lax.axis_index("wide")
    n = lax.axis_index("narrow")
    bx, bz, _ = rhs.shape
    hx, hz = bx // 2, bz // 2
    own_z = pl.ds(DEEP, bz)
    own_x = pl.ds(SIDE, bx)
    tiles_own = hz // 2
    f32 = jnp.float32

    loads = [pltpu.make_async_copy(ref, ins.at[i], in_sem.at[i]) for i, ref in enumerate((cond, rhs, guess))]
    for load in loads:
        load.start()

    def valid(dw):
        return (w + dw >= 0) & (w + dw < wide)

    def when(cond_, body):
        if cond_ is True:
            body()
        else:
            pl.when(cond_)(body)

    barrier = pltpu.get_barrier_semaphore()

    def greet(dev):
        pl.semaphore_signal(barrier, inc=1, device_id=dev, device_id_type=MESH)

    for j in range(1, narrow):
        greet((w, lax.rem(n + j, narrow)))
    for dw in (-1, 1):
        @pl.when(valid(dw))
        def _(dw=dw):
            for j in range(narrow):
                greet((w + dw, lax.rem(n + j, narrow)))

    @pl.loop(0, wide)
    def _(other):
        @pl.when((other < w - 1) | (other > w + 1))
        def _():
            greet((other, n))

    def clear(ref):
        ref[...] = jnp.zeros(ref.shape, f32)

    lower, upper = pl.ds(0, SIDE), pl.ds(SIDE + bx, SIDE)
    clear(p0.at[:, :, lower])
    clear(p0.at[:, :, upper])
    pl.when(n == 0)(lambda: clear(p0.at[:, pl.ds(0, DEEP), own_x]))
    pl.when(n == narrow - 1)(lambda: clear(p0.at[:, pl.ds(DEEP + bz, DEEP), own_x]))
    for at, dw in ((0, -1), (SIDE + hx, 1)):
        @pl.when(jnp.logical_not(valid(dw)))
        def _(at=at):
            clear(a1.at[:, :, pl.ds(at, SIDE)])
            clear(u1r.at[:, pl.ds(at, SIDE)])
    clear(u1.at[pl.ds(0, PAD)])
    clear(u1.at[pl.ds(PAD + u1r.shape[0], PAD)])

    for i in range(3):
        loads[i].wait()
        for z in range(bz):
            p0[i, DEEP + z, SIDE:SIDE + bx, :] = ins[i, :, z, :]

    def to_level_1(index, slices, factor):
        pairs = beside_each([slices[2 * i] + slices[2 * i + 1] for i in range(hz)])
        thin = map_rows(down_rows(bx), pairs)
        flat = stacked([thin[:, 2 * LANES * tt:2 * LANES * (tt + 1)] for tt in range(tiles_own)])
        done = factor * map_lanes(flat, down0[...])
        for tt in range(tiles_own):
            a1[index, n * tiles_own + tt, SIDE:SIDE + hx, :] = done[hx * tt:hx * (tt + 1)]

    zs = {1: (DEEP + bz - DEEP, 0, DEEP), -1: (DEEP, DEEP + bz, DEEP), 0: (DEEP, DEEP, bz)}
    xs = {1: (SIDE + bx - SIDE, 0, SIDE), -1: (SIDE, SIDE + bx, SIDE), 0: (SIDE, SIDE, bx)}
    around = [(1, 0), (-1, 0), (1, 1), (1, -1), (-1, 1), (-1, -1), (0, 1), (0, -1)]

    def has(dw, dn):
        good = None
        if dw:
            good = valid(dw)
        if dn:
            zgood = (n + dn >= 0) & (n + dn < narrow)
            good = zgood if good is None else good & zgood
        return good

    def mine_x(dw, dx):
        return bx - dx if dw == 1 else dx - 1

    def there_x(dw, dx):
        return SIDE - dx if dw == -1 else SIDE + bx + dx - 1

    def pairs(count):
        return [tuple(range(dx, min(dx + 2, count + 1))) for dx in range(1, count + 1, 2)]

    def run(dw, count, place):
        return min(place(dw, 1), place(dw, count))

    corners = [(-1, -1), (-1, 1), (1, -1), (1, 1)]
    parts = [(0, dz, DEEP - dz) for dz in range(1, DEEP)] + [(1, dz, DEEP - 1 - dz) for dz in range(1, DEEP - 1)]
    slots = []
    used = 0
    for i, dz, count in parts:
        slots.append((i, dz, count, used))
        used += count
    doubles = []
    for dz in range(1, DEEP):
        for pair in pairs(DEEP - dz):
            doubles.append((dz, pair, used))
            used += 1

    for c, (dw, dn) in enumerate(corners):
        for i, dz, count, at in slots:
            z = bz - dz if dn == 1 else dz - 1
            x = run(dw, count, mine_x)
            corner_out[c, at:at + count, :] = ins[i, x:x + count, z, :]
        for dz, pair, at in doubles:
            z = bz - dz if dn == 1 else dz - 1
            x = mine_x(dw, pair[0])
            row = ins[2, x, z:z + 1, :]
            if len(pair) > 1:
                odd = (iota((1, LANES), 1) + (x + z)) & 1
                row = jnp.where(odd == 1, row, ins[2, mine_x(dw, pair[1]), z:z + 1, :])
            corner_out[c, at:at + 1, :] = row

    for d, dw in enumerate((-1, 1)):
        x = run(dw, DEEP - 1, mine_x)
        side_out[d, 0:DEEP - 1] = ins[1, x:x + DEEP - 1]
        for at, pair in enumerate(pairs(DEEP)):
            x = mine_x(dw, pair[0])
            layer = ins[2, x]
            if len(pair) > 1:
                odd = (iota(layer.shape, 0) + iota(layer.shape, 1) + x) & 1
                layer = jnp.where(odd == 1, layer, ins[2, mine_x(dw, pair[1])])
            side_out[d, DEEP - 1 + at] = layer

    def corner_unpack(dw, dn):
        c = corners.index((-dw, -dn))
        for i, dz, count, at in slots:
            z = DEEP - dz if dn == -1 else DEEP + bz + dz - 1
            x = run(dw, count, there_x)
            p0[i, z, x:x + count, :] = corner_in[c, at:at + count, :]
        for dz, pair, at in doubles:
            z = DEEP - dz if dn == -1 else DEEP + bz + dz - 1
            for dx in pair:
                x = there_x(dw, dx)
                p0[2, z, x:x + 1, :] = corner_in[c, at:at + 1, :]

    def side_unpack(which, dw):
        d = (dw + 1) // 2
        if which == 0:
            x = run(dw, DEEP, there_x)
            for z in range(bz):
                p0[0, DEEP + z, x:x + DEEP, :] = k_in[d, :, z, :]
            return
        x = run(dw, DEEP - 1, there_x)
        for z in range(bz):
            p0[1, DEEP + z, x:x + DEEP - 1, :] = side_in[d, 0:DEEP - 1, z, :]
        for at, pair in enumerate(pairs(DEEP)):
            for dx in pair:
                x = there_x(dw, dx)
                p0[2, DEEP:DEEP + bz, x, :] = side_in[d, DEEP - 1 + at]

    def fine_refs(which, dw, dn):
        if which < 2 and dw and dn:
            c = corners.index((dw, dn))
            return corner_out.at[c], corner_in.at[c]
        arrays = (pl.ds(0, 1), pl.ds(1, 2), None)[which]
        if which == 0 and dw:
            return ins.at[0, pl.ds(run(dw, DEEP, mine_x), DEEP)], k_in.at[(1 - dw) // 2]
        if which == 1 and dw:
            return side_out.at[(dw + 1) // 2], side_in.at[(1 - dw) // 2]
        src_z, dst_z, len_z = zs[dn]
        src_x, dst_x, len_x = xs[dw]
        ref = u0r if which == 2 else p0
        lead = () if which == 2 else (arrays,)
        return (ref.at[lead + (pl.ds(src_z, len_z), pl.ds(src_x, len_x))],
                ref.at[lead + (pl.ds(dst_z, len_z), pl.ds(dst_x, len_x))])

    def fine(which, dw, dn):
        src, dst = fine_refs(which, dw, dn)
        mine = (dw + 1) * 3 + dn + 1
        theirs = (1 - dw) * 3 + 1 - dn
        return pltpu.make_async_remote_copy(
            src_ref=src, dst_ref=dst, send_sem=send0.at[which, mine], recv_sem=recv0.at[which, theirs],
            device_id=(w + dw, n + dn), device_id_type=MESH)

    def fine_in(which, dw, dn):
        _, dst = fine_refs(which, -dw, -dn)
        mine = (dw + 1) * 3 + dn + 1
        return pltpu.make_async_remote_copy(
            src_ref=dst, dst_ref=dst, send_sem=send0.at[which, mine], recv_sem=recv0.at[which, mine],
            device_id=(w + dw, n + dn), device_id_type=MESH)

    def fine_each(which, fun):
        for dw, dn in around:
            if which != 1 or not (dw and dn):
                pl.when(has(dw, dn))(lambda dw=dw, dn=dn: fun(dw, dn))

    def fine_start(which):
        fine_each(which, lambda dw, dn: fine(which, dw, dn).start())

    def fine_recv(which):
        def take(dw, dn):
            fine_in(which, dw, dn).wait_recv()
            if which < 2 and dw and dn:
                corner_unpack(dw, dn)
            elif which < 2 and dw:
                side_unpack(which, dw)
        fine_each(which, take)

    def fine_sent(which):
        fine_each(which, lambda dw, dn: fine(which, dw, dn).wait_send())

    def mid_ref(which):
        return u1r if which == 2 else a1.at[which]

    def middle(which, dw, j):
        ref = mid_ref(which)
        tile = pl.ds(n * tiles_own, tiles_own)
        return pltpu.make_async_remote_copy(
            src_ref=ref.at[tile, pl.ds(SIDE, hx)], dst_ref=ref.at[tile, pl.ds(SIDE - dw * hx, hx)],
            send_sem=send1.at[which, dw + 1], recv_sem=recv1.at[which, 1 - dw],
            device_id=(w + dw, lax.rem(n + j, narrow)), device_id_type=MESH)

    def middle_all(which, dw):
        count = narrow if dw else narrow - 1
        every = mid_ref(which).at[pl.ds(0, count * tiles_own), pl.ds(SIDE + dw * hx, hx)]
        return pltpu.make_async_remote_copy(
            src_ref=every, dst_ref=every, send_sem=send1.at[which, dw + 1], recv_sem=recv1.at[which, dw + 1],
            device_id=(w + dw, lax.rem(n + 1, narrow)), device_id_type=MESH)

    def mid_start(which):
        for dw in (-1, 1):
            @pl.when(valid(dw))
            def _(dw=dw):
                for j in range(narrow):
                    middle(which, dw, j).start()
        for j in range(1, narrow):
            middle(which, 0, j).start()

    def mid_recv(which):
        middle_all(which, 0).wait_recv()
        for dw in (-1, 1):
            pl.when(valid(dw))(lambda dw=dw: middle_all(which, dw).wait_recv())

    def mid_sent(which):
        middle_all(which, 0).wait_send()
        for dw in (-1, 1):
            pl.when(valid(dw))(lambda dw=dw: middle_all(which, dw).wait_send())

    def top(which, step):
        other = lax.rem(w + step, wide)
        return pltpu.make_async_remote_copy(
            src_ref=own2.at[which], dst_ref=g2.at[which, w], send_sem=send2.at[which],
            recv_sem=recv2.at[which], device_id=(other, n), device_id_type=MESH)

    def top_all(which):
        every = g2.at[which, pl.ds(0, wide - 1)]
        return pltpu.make_async_remote_copy(
            src_ref=every, dst_ref=every, send_sem=send2.at[which], recv_sem=recv2.at[which],
            device_id=(lax.rem(w + 1, wide), n), device_id_type=MESH)

    def top_start(which):
        @pl.loop(1, wide)
        def _(step):
            top(which, step).start()

    near = jnp.where(w > 0, 1, 0) + jnp.where(w < wide - 1, 1, 0)
    pl.semaphore_wait(barrier, (wide - 1 - near) + near * narrow + narrow - 1)

    fine_start(0)
    fine_start(1)
    for dw, dn in around:
        pl.when(jnp.logical_not(has(dw, dn)))(lambda dw=dw, dn=dn: clear(fine_refs(2, -dw, -dn)[1]))

    names = range(6)
    ny1, ny2, ny3 = LANES // 2, LANES // 4, LANES // 8
    tiles2 = a1.shape[1] // 4
    bf16 = jnp.bfloat16
    down0[...] = stacked([down_lanes(i, LANES) for i in (0, 2)]).astype(bf16)
    up0[...] = beside_each([up_lanes(i, LANES) for i in (0, 2)]).astype(bf16)
    down1[...] = stacked([down_lanes(i, ny1) for i in range(4)]).astype(bf16)
    up1[...] = beside_each([up_lanes(i, ny1) for i in range(4)]).astype(bf16)
    down2[...] = stacked([down_lanes(i, ny2) for i in range(tiles2)]).astype(bf16)
    up2[...] = beside_each([up_lanes(i, ny2) for i in range(tiles2)]).astype(bf16)
    to_level_1(0, [p0[0, DEEP + z, SIDE:SIDE + bx, :] for z in range(bz)], 0.125)
    fine_recv(0)
    zero_level = Level(p0.at[0], p0.at[1], p0.at[2], *[op0.at[i] for i in names], LANES, 1, 2 * DEEP + bz - 1, odd=1)
    zero_level.operator()
    fine_recv(1)
    mid_start(0)
    fine_sent(0)
    fine_sent(1)
    zero_level.smooth()
    to_level_1(1, [v[SIDE:SIDE + bx] for v in zero_level.defects(DEEP, DEEP + bz)], 0.5)
    mid_start(1)
    u0r[own_z, own_x, :] = p0[2, own_z, own_x, :]

    mid_recv(0)
    one_level = Level(a1.at[0], a1.at[1], u1, *[op1.at[i] for i in names], ny1, 0, a1.shape[1], off=PAD)
    rows2 = hx // 2

    def to_level_2(which, tiles, factor):
        flat = stacked([beside_each(tiles[4 * big:4 * big + 4]) for big in range(tiles2)])
        pack = factor * map_rows(down_rows(tiles2 * hx), map_lanes(flat, down1[...]))
        own2[which] = pack
        g2[which, w] = pack

    to_level_2(0, [a1[0, t, SIDE:SIDE + hx, :] for t in range(a1.shape[1])], 0.125)
    top_start(0)
    one_level.operator()
    mid_recv(1)
    one_level.smooth(blank=True)
    to_level_2(1, [v[SIDE:SIDE + hx] for v in one_level.defects(0, a1.shape[1])], 0.5)
    top_start(1)
    u1r[pl.ds(n * tiles_own, tiles_own), SIDE:SIDE + hx, :] = u1[pl.ds(PAD + n * tiles_own, tiles_own), SIDE:SIDE + hx, :]

    def unpack(which):
        for other in range(wide):
            for t in range(tiles2):
                a2[which, t, other * rows2:(other + 1) * rows2, :] = g2[which, other, t * rows2:(t + 1) * rows2, :]

    top_all(0).wait_recv()
    unpack(0)
    two_level = Level(a2.at[0], a2.at[1], u2, *[op2.at[i] for i in names], ny2, 0, tiles2)
    two_level.operator()
    all2, all3 = a2.shape[2], a3.shape[2]

    def to_level_3(tiles, factor):
        return factor * map_rows(down_rows(all2), map_lanes(beside_each(tiles), down2[...]))

    a3[0, 0] = to_level_3([a2[0, t] for t in range(tiles2)], 0.125)
    last = Level(a3.at[0], a3.at[1], a3.at[1], *[op3.at[i] for i in names], ny3, 0, 1)
    last.operator()
    mid_sent(0)
    mid_sent(1)
    top_all(0).wait_send()
    top_all(1).wait_recv()
    mid_start(2)
    fine_start(2)
    unpack(1)
    two_level.smooth(blank=True)
    source = to_level_3(two_level.defects(0, tiles2), 0.5)

    def image(v):
        spun = last.spin(v)
        return last.diag[0] * v - last.beside(0, v, spun, spun, spun)

    def total(v):
        return jnp.broadcast_to(jnp.sum(jnp.sum(v, axis=0, keepdims=True), axis=1, keepdims=True), (8, LANES))

    def tall(v):
        return jnp.concatenate([v] * (all3 // 8), axis=0)

    def advance(step, carry):
        answer, remain, wave, search, moved, twice, norm_inverse, rate = carry
        norm = total(remain * remain)
        cross = total(wave * remain)
        ahead = image(wave)
        beta = norm * norm_inverse
        below = cross - beta * (norm * rate)
        alpha = tall(norm / below)
        beta = tall(beta)
        norm_inverse = 1.0 / norm
        rate = below * norm_inverse
        twice = ahead + beta * twice
        moved = wave + beta * moved
        search = remain + beta * search
        answer = answer + alpha * search
        remain = remain - alpha * moved
        wave = wave - alpha * twice
        return answer, remain, wave, search, moved, twice, norm_inverse, rate

    nothing = jnp.zeros_like(source)
    short = jnp.zeros((8, LANES), f32)
    carry = (nothing, source, image(source), nothing, nothing, nothing, short, short)
    solved = lax.fori_loop(0, ITERS, advance, carry)[0]

    wider = map_lanes(map_rows(up_rows(all2, all3, 0), solved), up2[...])
    for t in range(tiles2):
        u2[t] = u2[t] + wider[:, LANES * t:LANES * (t + 1)]
    two_level.smooth()

    window = a1.shape[2]
    pick = up_rows(window, all2, w * rows2 - SIDE // 2)
    thin = map_rows(pick, beside_each([u2[t] for t in range(tiles2)]))
    grown = map_lanes(stacked([thin[:, LANES * t:LANES * (t + 1)] for t in range(tiles2)]), up1[...])
    top_all(1).wait_send()
    mid_sent(2)
    mid_recv(2)
    for t in range(a1.shape[1]):
        big, i = t // 4, t % 4
        u1[PAD + t] = u1r[t] + grown[window * big:window * (big + 1), LANES * i:LANES * (i + 1)]
    one_level.smooth()

    pick0 = up_rows(bx + 2 * SIDE, window, SIDE // 2)
    low, high = -DEEP // 4, (bz + DEEP - 1) // 4
    thin = map_rows(pick0, beside_each([u1[PAD + n * tiles_own + key] for key in range(low, high + 1)]))
    span = thin.shape[0]
    grown = map_lanes(stacked([thin[:, LANES * t:LANES * (t + 1)] for t in range(high + 1 - low)]), up0[...])
    fine_sent(2)
    fine_recv(2)
    for zi in range(2 * DEEP + bz):
        t = (zi - DEEP) // 4 - low
        side = ((zi - DEEP) % 4) // 2
        p0[2, zi] = u0r[zi] + grown[span * t:span * (t + 1), LANES * side:LANES * (side + 1)]
    zero_level.smooth()
    for z, left in enumerate(zero_level.defects(DEEP, DEEP + bz)):
        pressure[:, z, :] = p0[2, DEEP + z, SIDE:SIDE + bx, :]
        residual[:, z, :] = left[SIDE:SIDE + bx]


def local(wide, narrow, rhs, coefficient, guess):
    bx, bz, by = rhs.shape
    hx = bx // 2
    z0 = bz + 2 * DEEP
    x0 = bx + 2 * SIDE
    t1 = narrow * bz // 4
    x1 = hx + 2 * SIDE
    t2 = t1 // 4
    x2 = wide * bx // 4
    x3 = x2 // 2
    vmem = lambda *shape: pltpu.VMEM(shape, jnp.float32)
    layers = DEEP - 1 + (DEEP + 1) // 2
    half = lambda *shape: pltpu.VMEM(shape, jnp.bfloat16)
    dma = lambda *shape: pltpu.SemaphoreType.DMA(shape)
    out = jax.ShapeDtypeStruct(rhs.shape, jnp.float32)
    return pl.pallas_call(
        functools.partial(kernel, wide, narrow),
        out_shape=(out, out),
        in_specs=[pl.BlockSpec(memory_space=pltpu.HBM)] * 3,
        out_specs=[pl.BlockSpec(memory_space=pltpu.VMEM)] * 2,
        scratch_shapes=[
            vmem(3, bx, bz, by), vmem(4, 24, LANES), vmem(4, 24, LANES),
            vmem(2, DEEP, bz, by), vmem(2, layers, bz, by), vmem(2, layers, bz, by),
            vmem(3, z0, x0, by), vmem(z0, x0, by), vmem(6, z0, x0, by),
            vmem(2, t1, x1, LANES), vmem(t1, x1, LANES), vmem(t1 + 2 * PAD, x1, LANES), vmem(6, t1, x1, LANES),
            vmem(2, t2, x2, LANES), vmem(2, t2 * hx // 2, LANES), vmem(2, wide, t2 * hx // 2, LANES),
            vmem(t2, x2, LANES), vmem(6, t2, x2, LANES),
            vmem(2, 1, x3, LANES), vmem(6, 1, x3, LANES),
            half(2 * LANES, LANES), half(LANES, 2 * LANES), half(4 * LANES, LANES), half(LANES, 4 * LANES),
            half(t2 * LANES, LANES), half(LANES, t2 * LANES),
            dma(3), dma(3, 9), dma(3, 9), dma(3, 3), dma(3, 3), dma(2), dma(2),
        ],
        compiler_params=pltpu.CompilerParams(collective_id=0, has_side_effects=True, vmem_limit_bytes=48 * 2**20),
    )(*[pltpu.with_memory_space_constraint(a, pltpu.HBM) for a in (rhs, coefficient, guess)])


def solution(mesh):
    spec = P("wide", "narrow", None)
    return jax.shard_map(
        functools.partial(local, mesh.shape["wide"], mesh.shape["narrow"]),
        mesh=mesh,
        in_specs=(spec, spec, spec),
        out_specs=(spec, spec),
        check_vma=False,
    )
```
